256 devices in a mesh: dp: 32 (over x, y, core), tensor: 8 (over z).
Axes of the slice: x: 4, y: 4, z: 8, core: 2. Of those that a mesh axis runs over, the one named last changes fastest.
Arguments:
- momentum: float32 [32, 5120, 1024], P('dp', None, 'tensor'), may hold values from -6 to 6
- activations: bfloat16 [32768, 5120], P(('dp', 'tensor')), may hold values from -6 to 6
- out_grads: bfloat16 [32768, 1024], P('dp', 'tensor'), may hold values from -0.29882812 to 0.29882812
- positions: int32 [32, 16, 4, 5120], P('dp', 'tensor'), may hold values from 0 to 63, as said below
Outputs:
- new_momentum: float32 [32, 5120, 1024], P('dp', None, 'tensor')
- update: bfloat16 [5120, 1024], P(None, 'tensor')
The draws below stay inside these ranges and needn't reach their ends.
Inputs may be any that keep to these rules, and one draw needn't show every extreme that they name: The 4 positions of one block of one row of one replica are all different.
All inputs are finite; a program needn't handle non-finite values.
Results may differ from the reference program's by a relative error of at most 0.00075.
Values may be sent and summed in bfloat16 or wider, within the bound.
A program may use at most 128 MiB of HBM per device.

```python
import jax
import jax.numpy as jnp
from jax import lax

D = 5120
KVW = 1024
SPAN = 64
PICKS = 4
TOK_DEV = 128
TOKENS = 32768
BLOCKS_ROW = 16
N_DP = 32
N_TENSOR = 8


def draw_positions(key, part):
    first_key, second_key = jax.random.split(jax.random.fold_in(key, 17))
    width = SPAN // PICKS
    base = jax.random.randint(first_key, (N_DP, BLOCKS_ROW, 1, D), 0, SPAN)
    offsets = jax.random.randint(second_key, (N_DP, BLOCKS_ROW, PICKS, D), 0, width)
    windows = width * jnp.arange(PICKS, dtype=jnp.int32)[None, None, :, None]
    return ((base + windows + offsets) % SPAN).astype(jnp.int32)


def block_levels(stream_key, extent, pieces, smallest, high):
    level = 1.0
    for position, blocks in pieces:
        draws = jax.random.uniform(jax.random.fold_in(jax.random.fold_in(stream_key, 6), position), (blocks,), jnp.float32, smallest / len(pieces), high / len(pieces))
        level = level * jnp.repeat(jnp.exp(draws), extent[position] // blocks).reshape((-1,) + (1,) * (len(extent) - 1 - position))
    return level


def centred(key, shape, scale, reach, pieces=(), kind=jnp.bfloat16):
    entries = jax.random.normal(key, shape, jnp.float32) * scale
    if len(pieces) > 0:
        entries = block_levels(key, shape, pieces, -0.22, 0.18) * entries
    return jnp.clip(entries, min=-reach, max=reach).astype(kind)


def setup_inputs(seed: int = 0) -> dict:
    key_list = jax.random.split(jax.random.key(seed), 5)
    return {
        "momentum": centred(key_list[0], (N_DP, D, KVW), 1.0, 6.0, ((0, 32), (2, 8)), jnp.float32),
        "activations": centred(key_list[1], (TOKENS, D), 1.0, 6.0, ((0, 256),)),
        "out_grads": centred(key_list[2], (TOKENS, KVW), 0.05, 0.29882812, ((0, 32), (1, 8))),
        "positions": draw_positions(jax.random.fold_in(key_list[4], 71), 0),
    }


def dct_table():
    freq = jnp.arange(64, dtype=jnp.float32)[:, None]
    place = jnp.arange(64, dtype=jnp.float32)[None, :]
    scales = jnp.where(freq == 0, jnp.float32(1.0 / 8.0), jnp.float32((2.0 / 64.0) ** 0.5))
    return scales * jnp.cos(jnp.float32(jnp.pi) * (2.0 * place + 1.0) * freq / 128.0)

def reference(momentum, activations, out_grads, positions):
    cosines = dct_table()
    inputs_rep = activations.reshape(N_DP, TOK_DEV * N_TENSOR, D)
    grads_rep = out_grads.reshape(N_DP, TOK_DEV * N_TENSOR, KVW)
    lane_ids = jnp.arange(64, dtype=jnp.int32)

    def per_replica(summed, record):
        moment_one, inputs_one, grads_one, picks_one = record
        gradient = jnp.dot(inputs_one.T, grads_one, preferred_element_type=jnp.float32)
        accumulated = 0.9 * moment_one + gradient
        coeffs = jnp.dot(accumulated.reshape(-1, 64), cosines.T, precision=lax.Precision.HIGHEST)
        coeffs = coeffs.reshape(D, KVW // 64, 64)
        hits = jnp.where(picks_one[:, :, None, :] == lane_ids[None, None, :, None], 1.0, 0.0)
        chosen = lax.optimization_barrier(jnp.sum(hits, axis=1)).transpose(2, 0, 1).astype(coeffs.dtype)
        own_tile = coeffs * chosen
        restored = jnp.dot(own_tile.reshape(-1, 64), cosines, precision=lax.Precision.HIGHEST)
        return (summed + own_tile, accumulated - restored.reshape(D, KVW))
    start_sum = jnp.zeros((D, KVW // 64, 64), jnp.float32)
    summed, new_momentum = lax.scan(per_replica, start_sum, (momentum, inputs_rep, grads_rep, positions))
    decoded = jnp.dot(summed.reshape(-1, 64), cosines, precision=lax.Precision.HIGHEST).reshape(D, KVW)
    row_scale = jnp.sqrt(lax.optimization_barrier(jnp.mean(decoded * decoded, axis=1, keepdims=True)) + 1e-05)
    update = (decoded / row_scale).astype(jnp.bfloat16)
    return (new_momentum, update)
```

```python
import functools

import jax
import jax.numpy as jnp
import numpy as np
from jax import lax
from jax.experimental import pallas as pl
from jax.experimental.pallas import tpu as pltpu
from jax.sharding import PartitionSpec as P

MESH = pl.DeviceIdType.MESH
HIGH = lax.Precision.HIGHEST
ROWS, COLS, TOK = 5120, 128, 128
NZ, NDP = 8, 32
CHUNK = 256
NQ = ROWS // CHUNK
TPC = CHUNK // 128
NT = ROWS // 128
SLOTS = -(-NT // NDP)

AT_FWD1, AT_FWD2, AT_SUM, AT_PASS, AT_FINISH, AT_OWN1, AT_OWN2 = 2, 4, 6, 8, 10, 11, 12


def dct_blocks():
    freq = np.arange(64, dtype=np.float64)[:, None]
    place = np.arange(64, dtype=np.float64)[None, :]
    scales = np.where(freq == 0, 1.0 / 8.0, np.sqrt(2.0 / 64.0))
    table = scales * np.cos(np.pi * (2.0 * place + 1.0) * freq / 128.0)
    return np.kron(np.eye(COLS // 64), table).astype(np.float32)


def kernel(
    a_ref, m_ref, g_ref, pos_ref, dct_ref, inv_ref,
    nm_ref, upd_ref,
    abuf, gown, gnear, gsum, mbuf, nmbuf, sout, scout, sbuf, scin,
    msg, rx, dec, sqs, ust,
    loc_sem, m_sem, nm_sem, raw_ss, raw_rs, g_ss, g_rs,
    sum_ss, sum_rs, pass_ss, msg_ss, rx_rs, sq_ss, sq_rs, up_ss, up_rs, ul_sem,
):
    me = lax.axis_index("dp")
    z = lax.axis_index("tensor")
    right = lax.rem(z + 1, NZ)
    left = lax.rem(z + NZ - 1, NZ)

    def place(q):
        return lax.rem(z + 4 - lax.rem(q, 4), 4)

    def cols(q):
        return pl.ds(pl.multiple_of(q * CHUNK, CHUNK), CHUNK)

    def owner(t):
        return lax.rem(t * 5, NDP)

    def mom_in(q):
        return pltpu.make_async_copy(m_ref.at[cols(q)], mbuf.at[q], m_sem.at[q])

    def mom_out(q):
        return pltpu.make_async_copy(nmbuf.at[q], nm_ref.at[cols(q)], nm_sem.at[q])

    def own_local(q, u):
        return pltpu.make_async_copy(a_ref.at[:, cols(q)], abuf.at[q, u], loc_sem.at[q])

    def raw(q, p, way, slot, own=False):
        return pltpu.make_async_remote_copy(
            src_ref=a_ref.at[:, cols(q)] if own else abuf.at[q, p],
            dst_ref=abuf.at[q, p],
            send_sem=raw_ss.at[q, way, slot],
            recv_sem=raw_rs.at[q, p],
            device_id={"tensor": left if way else right},
            device_id_type=MESH,
        )

    def grads(end, c, p):
        target = lax.rem(z + (NZ - 1 - c if end else 1 + c), NZ)
        block = lax.rem(target + (NZ - 3 if end else 0) + p, NZ)
        return pltpu.make_async_remote_copy(
            src_ref=g_ref.at[pl.ds(pl.multiple_of(block * TOK, TOK), TOK)],
            dst_ref=gnear.at[end, c, p],
            send_sem=g_ss.at[end, c, p],
            recv_sem=g_rs.at[end, c, p],
            device_id={"tensor": target},
            device_id_type=MESH,
        )

    def sums(q, target):
        return (
            pltpu.make_async_remote_copy(
                src_ref=sout.at[q], dst_ref=sbuf.at[q],
                send_sem=sum_ss.at[q, 0], recv_sem=sum_rs.at[q, 0],
                device_id={"tensor": target}, device_id_type=MESH,
            ),
            pltpu.make_async_remote_copy(
                src_ref=scout.at[q], dst_ref=scin.at[q],
                send_sem=sum_ss.at[q, 1], recv_sem=sum_rs.at[q, 1],
                device_id={"tensor": target}, device_id_type=MESH,
            ),
        )

    def passed(q, target):
        return (
            pltpu.make_async_remote_copy(
                src_ref=sbuf.at[q, 1], dst_ref=sbuf.at[q, 1],
                send_sem=pass_ss.at[q, 0], recv_sem=sum_rs.at[q, 0],
                device_id={"tensor": target}, device_id_type=MESH,
            ),
            pltpu.make_async_remote_copy(
                src_ref=scin.at[q], dst_ref=scin.at[q],
                send_sem=pass_ss.at[q, 1], recv_sem=sum_rs.at[q, 1],
                device_id={"tensor": target}, device_id_type=MESH,
            ),
        )

    def picks(t, source, target):
        slot = lax.div(t, NDP)
        return pltpu.make_async_remote_copy(
            src_ref=msg.at[t], dst_ref=rx.at[slot, source],
            send_sem=msg_ss.at[t], recv_sem=rx_rs.at[slot, source],
            device_id={"dp": target}, device_id_type=MESH,
        )

    def squares(slot, source, target):
        return pltpu.make_async_remote_copy(
            src_ref=sqs.at[slot, z], dst_ref=sqs.at[slot, source],
            send_sem=sq_ss.at[slot, target], recv_sem=sq_rs.at[slot, source],
            device_id={"tensor": target}, device_id_type=MESH,
        )

    def tile(t):
        return pl.ds(pl.multiple_of(t * 128, 128), 128)

    def spread(t, target):
        slot = lax.div(t, NDP)
        return pltpu.make_async_remote_copy(
            src_ref=ust.at[slot], dst_ref=upd_ref.at[tile(t)],
            send_sem=up_ss.at[slot, target], recv_sem=up_rs.at[t],
            device_id={"dp": target}, device_id_type=MESH,
        )

    def keep(t):
        slot = lax.div(t, NDP)
        return pltpu.make_async_copy(ust.at[slot], upd_ref.at[tile(t)], ul_sem.at[slot])

    def start_mom(q, _):
        mom_in(q).start()
        return 0

    lax.fori_loop(0, NQ, start_mom, 0)
    barrier = pltpu.get_barrier_semaphore()

    def greet_z(d, _):
        pl.semaphore_signal(
            barrier, inc=1, device_id={"tensor": lax.rem(z + d, NZ)}, device_id_type=MESH
        )
        return 0

    def greet_dp(d, _):
        pl.semaphore_signal(
            barrier, inc=1, device_id={"dp": lax.rem(me + d, NDP)}, device_id_type=MESH
        )
        return 0

    lax.fori_loop(1, NZ, greet_z, 0)
    lax.fori_loop(1, NDP, greet_dp, 0)
    for b in range(NZ + 3):
        block = g_ref[(b % NZ) * TOK:(b % NZ + 1) * TOK, :]
        gown[:, b * TOK:(b + 1) * TOK] = block.T
    pl.semaphore_wait(barrier, NZ + NDP - 2)

    def send_own(q):
        u = place(q)
        own_local(q, u).start()

        @pl.when(u <= 2)
        def _():
            raw(q, u, 0, 0, own=True).start()

        @pl.when(u >= 1)
        def _():
            raw(q, u, 1, 0, own=True).start()

    def send_grads():
        for c in range(2):
            for p in range(4):
                for end in range(2):
                    grads(end, c, p).start()

    def forward1(q):
        u = place(q)

        @pl.when((u == 1) | (u == 2))
        def _():
            raw(q, u - 1, 0, 1).wait_recv()
            raw(q, u - 1, 0, 1).start()
            raw(q, u + 1, 1, 1).wait_recv()
            raw(q, u + 1, 1, 1).start()

    def forward2(q):
        u = place(q)

        @pl.when(u == 2)
        def _():
            raw(q, 0, 0, 2).wait_recv()
            raw(q, 0, 0, 2).start()

        @pl.when(u == 1)
        def _():
            raw(q, 3, 1, 2).wait_recv()
            raw(q, 3, 1, 2).start()

    def make_sums(q):
        u = place(q)
        own_local(q, u).wait()

        @pl.when((u == 0) | (u == 3))
        def _():
            for p in range(4):
                @pl.when(u != p)
                def _():
                    raw(q, p, 0, 0).wait_recv()
            end = lax.div(u, 3)
            far = jnp.dot(
                gsum[end], abuf[q].reshape(4 * TOK, CHUNK), preferred_element_type=jnp.float32
            )
            for c in range(2):
                part = far[c * COLS:(c + 1) * COLS]
                top = jnp.maximum(jnp.max(jnp.abs(part), axis=0, keepdims=True), 1e-30)
                sout[q, c] = jnp.round(part * (32767.0 / top)).astype(jnp.int32).astype(jnp.int16)
                unit = top * (1.0 / 32767.0)
                for i in range(TPC):
                    scout[q, c * TPC + i:c * TPC + i + 1, :] = unit[:, i * 128:(i + 1) * 128]
            for copy in sums(q, lax.rem(z + NZ - 1 + 2 * end, NZ)):
                copy.start()

    def pass_sums(q):
        u = place(q)

        @pl.when((u == 0) | (u == 3))
        def _():
            end = lax.div(u, 3)
            for copy in sums(q, right):
                copy.wait_recv()
            for copy in passed(q, lax.rem(z + 1 + (NZ - 2) * end, NZ)):
                copy.start()

    def finish(q):
        u = place(q)
        inner = jnp.where((u == 1) | (u == 2), 1, 0)

        @pl.when(inner == 1)
        def _():
            for copy in passed(q, right):
                copy.wait_recv()

        mom_in(q).wait()
        first = lax.rem(z - u + NZ, NZ)
        near = jnp.dot(
            gown[:, pl.ds(pl.multiple_of(first * TOK, TOK), 4 * TOK)],
            abuf[q].reshape(4 * TOK, CHUNK),
            preferred_element_type=jnp.float32,
        )
        unit = jnp.concatenate(
            [scin[q, pl.ds(inner * TPC + i, 1), :] for i in range(TPC)], axis=1
        )
        accumulated = 0.9 * mbuf[q].T + (near + sbuf[q, inner].astype(jnp.float32) * unit)
        coeffs = jnp.dot(
            dct_ref[...], accumulated, precision=HIGH, preferred_element_type=jnp.float32
        )
        lanes = lax.broadcasted_iota(jnp.int32, (64, CHUNK), 0)
        kept = []
        for b in range(2):
            block = coeffs[b * 64:(b + 1) * 64]
            tile_b = jnp.zeros((64, CHUNK), jnp.float32)
            for j in range(4):
                where = pos_ref[b, j:j + 1, cols(q)]
                value = jnp.where(where == lanes, block, 0.0)
                tile_b = tile_b + value
                total = jnp.sum(value, axis=0, keepdims=True)
                spot = where.astype(jnp.float32)
                row = b * 4 + j
                for i in range(TPC):
                    part = slice(i * 128, (i + 1) * 128)
                    msg[q * TPC + i, row:row + 1, :] = total[:, part]
                    msg[q * TPC + i, row + 8:row + 9, :] = spot[:, part]
            kept.append(tile_b)

        def hand_over(i, _):
            t = q * TPC + i

            @pl.when(owner(t) == me)
            def _():
                rx[lax.div(t, NDP), me] = msg[t]

            @pl.when(owner(t) != me)
            def _():
                picks(t, me, owner(t)).start()

            return 0

        lax.fori_loop(0, TPC, hand_over, 0)
        restored = jnp.dot(
            inv_ref[...], jnp.concatenate(kept, axis=0), precision=HIGH,
            preferred_element_type=jnp.float32,
        )
        nmbuf[q] = (accumulated - restored).T
        mom_out(q).start()

    def own1(t):
        @pl.when(owner(t) == me)
        def _():
            slot = lax.div(t, NDP)

            def arrive(s, _):
                @pl.when(s != me)
                def _():
                    picks(t, s, lax.rem(me + 1, NDP)).wait_recv()
                return 0

            lax.fori_loop(0, NDP, arrive, 0)
            lanes = lax.broadcasted_iota(jnp.int32, (64, 128), 0).astype(jnp.float32)

            def add(s, totals):
                m = rx[slot, s]
                out = []
                for b in range(2):
                    total = totals[b]
                    for j in range(4):
                        row = b * 4 + j
                        total = total + jnp.where(
                            m[row + 8:row + 9] == lanes, m[row:row + 1], 0.0
                        )
                    out.append(total)
                return tuple(out)

            zero = jnp.zeros((64, 128), jnp.float32)
            totals = lax.fori_loop(0, NDP, add, (zero, zero))
            decoded = jnp.dot(
                inv_ref[...], jnp.concatenate(totals, axis=0), precision=HIGH,
                preferred_element_type=jnp.float32,
            )
            dec[slot] = decoded
            sqs[slot, z] = jnp.broadcast_to(
                jnp.sum(decoded * decoded, axis=0, keepdims=True), (8, 128)
            )

            def tell(d, _):
                squares(slot, z, lax.rem(z + d, NZ)).start()
                return 0

            lax.fori_loop(1, NZ, tell, 0)

    def own2(t):
        @pl.when(owner(t) == me)
        def _():
            slot = lax.div(t, NDP)

            def hear(d, _):
                squares(slot, lax.rem(z + d, NZ), lax.rem(z + d, NZ)).wait_recv()
                return 0

            lax.fori_loop(1, NZ, hear, 0)
            total = sqs[slot, 0, 0:1]
            for s in range(1, NZ):
                total = total + sqs[slot, s, 0:1]
            scale = jnp.sqrt(total * (1.0 / (COLS * NZ)) + 1e-05)
            ust[slot] = (dec[slot] / scale).T.astype(jnp.bfloat16)
            keep(t).start()

            def give(d, _):
                spread(t, lax.rem(me + d, NDP)).start()
                return 0

            lax.fori_loop(1, NDP, give, 0)

    def step(t, _):
        def stage(at, act):
            @pl.when((t >= at) & (t < at + NQ))
            def _():
                act(t - at)

        def tiles(act):
            def run(q):
                def one(i, _):
                    act(q * TPC + i)
                    return 0
                lax.fori_loop(0, TPC, one, 0)
            return run

        stage(AT_FWD1, forward1)
        stage(AT_FWD2, forward2)
        stage(AT_PASS, pass_sums)
        stage(0, send_own)

        @pl.when(t == 0)
        def _():
            send_grads()

        @pl.when(t == AT_SUM)
        def _():
            for end in range(2):
                for c in range(2):
                    for p in range(4):
                        grads(end, c, p).wait_recv()
                        gsum[end, c * COLS:(c + 1) * COLS, p * TOK:(p + 1) * TOK] = (
                            gnear[end, c, p].T
                        )

        stage(AT_SUM, make_sums)
        stage(AT_FINISH, finish)
        stage(AT_OWN1, tiles(own1))
        stage(AT_OWN2, tiles(own2))
        return 0

    lax.fori_loop(0, NQ + AT_OWN2, step, 0)

    for end in range(2):
        for c in range(2):
            for p in range(4):
                grads(end, c, p).wait_send()

    def drain(q, _):
        u = place(q)
        mom_out(q).wait()

        @pl.when(u <= 2)
        def _():
            raw(q, u, 0, 0, own=True).wait_send()

        @pl.when(u >= 1)
        def _():
            raw(q, u, 1, 0, own=True).wait_send()

        @pl.when((u == 1) | (u == 2))
        def _():
            raw(q, u - 1, 0, 1).wait_send()
            raw(q, u + 1, 1, 1).wait_send()

        @pl.when(u == 2)
        def _():
            raw(q, 0, 0, 2).wait_send()

        @pl.when(u == 1)
        def _():
            raw(q, 3, 1, 2).wait_send()

        @pl.when((u == 0) | (u == 3))
        def _():
            for copy in sums(q, right) + passed(q, right):
                copy.wait_send()
        return 0

    lax.fori_loop(0, NQ, drain, 0)

    def drain_tile(t, _):
        slot = lax.div(t, NDP)

        @pl.when(owner(t) == me)
        def _():
            keep(t).wait()

            def quiet(d, _):
                squares(slot, z, lax.rem(z + d, NZ)).wait_send()
                return 0

            lax.fori_loop(1, NZ, quiet, 0)

            def given(d, _):
                spread(t, lax.rem(me + d, NDP)).wait_send()
                return 0

            lax.fori_loop(1, NDP, given, 0)

        @pl.when(owner(t) != me)
        def _():
            picks(t, me, owner(t)).wait_send()
            spread(t, owner(t)).wait_recv()
        return 0

    lax.fori_loop(0, NT, drain_tile, 0)


def body(momentum, activations, out_grads, positions):
    blocks = dct_blocks()
    vmem = pl.BlockSpec(memory_space=pltpu.VMEM)
    anywhere = pl.BlockSpec(memory_space=pl.ANY)
    dma = pltpu.SemaphoreType.DMA
    new_momentum, update = pl.pallas_call(
        kernel,
        out_shape=(
            jax.ShapeDtypeStruct((ROWS, COLS), jnp.float32),
            jax.ShapeDtypeStruct((ROWS, COLS), jnp.bfloat16),
        ),
        in_specs=[anywhere, anywhere, vmem, vmem, vmem, vmem],
        out_specs=(anywhere, anywhere),
        scratch_shapes=[
            pltpu.VMEM((NQ, 4, TOK, CHUNK), jnp.bfloat16),
            pltpu.VMEM((COLS, (NZ + 3) * TOK), jnp.bfloat16),
            pltpu.VMEM((2, 2, 4, TOK, COLS), jnp.bfloat16),
            pltpu.VMEM((2, 2 * COLS, 4 * TOK), jnp.bfloat16),
            pltpu.VMEM((NQ, CHUNK, COLS), jnp.float32),
            pltpu.VMEM((NQ, CHUNK, COLS), jnp.float32),
            pltpu.VMEM((NQ, 2, COLS, CHUNK), jnp.int16),
            pltpu.VMEM((NQ, 8, 128), jnp.float32),
            pltpu.VMEM((NQ, 2, COLS, CHUNK), jnp.int16),
            pltpu.VMEM((NQ, 8, 128), jnp.float32),
            pltpu.VMEM((NT, 16, 128), jnp.float32),
            pltpu.VMEM((SLOTS, NDP, 16, 128), jnp.float32),
            pltpu.VMEM((SLOTS, COLS, 128), jnp.float32),
            pltpu.VMEM((SLOTS, NZ, 8, 128), jnp.float32),
            pltpu.VMEM((SLOTS, 128, COLS), jnp.bfloat16),
            dma((NQ,)), dma((NQ,)), dma((NQ,)),
            dma((NQ, 2, 3)), dma((NQ, 4)),
            dma((2, 2, 4)), dma((2, 2, 4)),
            dma((NQ, 2)), dma((NQ, 2)), dma((NQ, 2)),
            dma((NT,)), dma((SLOTS, NDP)),
            dma((SLOTS, NZ)), dma((SLOTS, NZ)),
            dma((SLOTS, NDP)), dma((NT,)), dma((SLOTS,)),
        ],
        compiler_params=pltpu.CompilerParams(
            collective_id=0, has_side_effects=True, vmem_limit_bytes=48 << 20
        ),
    )(activations, momentum[0], out_grads, positions[0], blocks, blocks.T)
    return new_momentum[None], update


def solution(mesh):
    placed = (
        P("dp", None, "tensor"),
        P(("dp", "tensor"), None),
        P("dp", "tensor"),
        P("dp", "tensor", None, None),
    )
    return jax.shard_map(
        body,
        mesh=mesh,
        in_specs=placed,
        out_specs=(P("dp", None, "tensor"), P(None, "tensor")),
        check_vma=False,
    )
```

```python
import functools

import jax
import jax.numpy as jnp
import numpy as np
from jax import lax
from jax.experimental import pallas as pl
from jax.experimental.pallas import tpu as pltpu
from jax.sharding import PartitionSpec as P

MESH = pl.DeviceIdType.MESH
HIGH = lax.Precision.HIGHEST
ROWS, COLS, TOK = 5120, 128, 128
NZ, NDP = 8, 32
CHUNK = 256
NQ = ROWS // CHUNK
TPC = CHUNK // 128
NT = ROWS // 128
SLOTS = -(-NT // NDP)

AT_FWD1, AT_FWD2, AT_SUM, AT_PASS, AT_FINISH = 3, 6, 9, 12, 14
AT_OWN1, AT_OWN2, AT_RELAY = 17, 22, 25


def dct_blocks():
    freq = np.arange(64, dtype=np.float64)[:, None]
    place = np.arange(64, dtype=np.float64)[None, :]
    scales = np.where(freq == 0, 1.0 / 8.0, np.sqrt(2.0 / 64.0))
    table = scales * np.cos(np.pi * (2.0 * place + 1.0) * freq / 128.0)
    return np.kron(np.eye(COLS // 64), table).astype(np.float32)


def kernel(
    a_ref, m_ref, g_ref, pos_hbm, dct_hbm,
    nm_ref, upd_ref,
    gall, pos_ref, dct_ref, inv_ref,
    abuf, gown, gnear, gsum, mbuf, nmbuf, sout, scout, sbuf, scin,
    msg, rx, dec, sqs, ust,
    loc_sem, m_sem, nm_sem, raw_ss, raw_rs, g_ss, g_rs,
    sum_ss, sum_rs, pass_ss, msg_ss, rx_rs, sq_ss, sq_rs, up_ss, up_rs, ul_sem, relay_ss, in_sem,
):
    me = lax.axis_index("dp")
    z = lax.axis_index("tensor")
    right = lax.rem(z + 1, NZ)
    left = lax.rem(z + NZ - 1, NZ)
    twin = me + 1 - 2 * lax.rem(me, 2)

    def place(q):
        return lax.rem(z + 4 - lax.rem(q, 4), 4)

    def cols(q):
        return pl.ds(pl.multiple_of(q * CHUNK, CHUNK), CHUNK)

    def owner(t):
        return lax.rem(t * 5, NDP)

    mom_in = pltpu.make_async_copy(m_ref, mbuf, m_sem)

    def mom_out(q):
        return pltpu.make_async_copy(nmbuf.at[q], nm_ref.at[cols(q)], nm_sem)

    def own_local(q):
        return pltpu.make_async_copy(a_ref.at[:, cols(q)], abuf.at[q, place(q)], loc_sem)

    def sent(ref, sem):
        pltpu.make_async_remote_copy(
            src_ref=ref, dst_ref=ref, send_sem=sem, recv_sem=sem,
            device_id={"tensor": right}, device_id_type=MESH,
        ).wait_send()

    def arrived(ref, sem):
        pltpu.make_async_remote_copy(
            src_ref=ref, dst_ref=ref, send_sem=sem, recv_sem=sem,
            device_id={"tensor": right}, device_id_type=MESH,
        ).wait_recv()

    def raw(q, p, way, own=False):
        return pltpu.make_async_remote_copy(
            src_ref=a_ref.at[:, cols(q)] if own else abuf.at[q, p],
            dst_ref=abuf.at[q, p],
            send_sem=raw_ss,
            recv_sem=raw_rs.at[q, p],
            device_id={"tensor": left if way else right},
            device_id_type=MESH,
        )

    def grads(end, c, p):
        target = lax.rem(z + (NZ - 1 - c if end else 1 + c), NZ)
        block = lax.rem(target + (NZ - 3 if end else 0) + p, NZ)
        return pltpu.make_async_remote_copy(
            src_ref=g_ref.at[pl.ds(pl.multiple_of(block * TOK, TOK), TOK)],
            dst_ref=gnear.at[end, c, p],
            send_sem=g_ss,
            recv_sem=g_rs,
            device_id={"tensor": target},
            device_id_type=MESH,
        )

    def sums(q, target):
        return (
            pltpu.make_async_remote_copy(
                src_ref=sout.at[q], dst_ref=sbuf.at[q],
                send_sem=sum_ss.at[0], recv_sem=sum_rs.at[q, 0],
                device_id={"tensor": target}, device_id_type=MESH,
            ),
            pltpu.make_async_remote_copy(
                src_ref=scout.at[q], dst_ref=scin.at[q],
                send_sem=sum_ss.at[1], recv_sem=sum_rs.at[q, 1],
                device_id={"tensor": target}, device_id_type=MESH,
            ),
        )

    def passed(q, target):
        return (
            pltpu.make_async_remote_copy(
                src_ref=sbuf.at[q, 1], dst_ref=sbuf.at[q, 1],
                send_sem=pass_ss.at[0], recv_sem=sum_rs.at[q, 0],
                device_id={"tensor": target}, device_id_type=MESH,
            ),
            pltpu.make_async_remote_copy(
                src_ref=scin.at[q], dst_ref=scin.at[q],
                send_sem=pass_ss.at[1], recv_sem=sum_rs.at[q, 1],
                device_id={"tensor": target}, device_id_type=MESH,
            ),
        )

    def picks(t, source, target):
        slot = lax.div(t, NDP)
        return pltpu.make_async_remote_copy(
            src_ref=msg.at[t], dst_ref=rx.at[slot, source],
            send_sem=msg_ss, recv_sem=rx_rs.at[slot],
            device_id={"dp": target}, device_id_type=MESH,
        )

    def squares(slot, source, target):
        return pltpu.make_async_remote_copy(
            src_ref=sqs.at[slot, z], dst_ref=sqs.at[slot, source],
            send_sem=sq_ss.at[slot], recv_sem=sq_rs.at[slot],
            device_id={"tensor": target}, device_id_type=MESH,
        )

    def tile(t):
        return pl.ds(pl.multiple_of(t * 128, 128), 128)

    def spread(t, target):
        slot = lax.div(t, NDP)
        return pltpu.make_async_remote_copy(
            src_ref=ust.at[slot], dst_ref=upd_ref.at[tile(t)],
            send_sem=up_ss.at[slot], recv_sem=up_rs.at[t],
            device_id={"dp": target}, device_id_type=MESH,
        )

    def onward(t):
        return pltpu.make_async_remote_copy(
            src_ref=upd_ref.at[tile(t)], dst_ref=upd_ref.at[tile(t)],
            send_sem=relay_ss, recv_sem=up_rs.at[t],
            device_id={"dp": twin}, device_id_type=MESH,
        )

    def keep(t):
        slot = lax.div(t, NDP)
        return pltpu.make_async_copy(ust.at[slot], upd_ref.at[tile(t)], ul_sem.at[slot])

    def start_own(q, _):
        own_local(q).start()
        return 0

    small = [
        pltpu.make_async_copy(source, target, in_sem.at[i])
        for i, (source, target) in enumerate(
            ((g_ref, gall), (pos_hbm, pos_ref), (dct_hbm, dct_ref))
        )
    ]
    for copy in small:
        copy.start()
    mom_in.start()
    lax.fori_loop(0, NQ, start_own, 0)
    barrier = pltpu.get_barrier_semaphore()

    def greet_z(d, _):
        pl.semaphore_signal(
            barrier, inc=1, device_id={"tensor": lax.rem(z + d, NZ)}, device_id_type=MESH
        )
        return 0

    def greet_dp(d, _):
        pl.semaphore_signal(
            barrier, inc=1, device_id={"dp": lax.rem(me + d, NDP)}, device_id_type=MESH
        )
        return 0

    lax.fori_loop(1, NZ, greet_z, 0)
    lax.fori_loop(1, NDP, greet_dp, 0)
    for copy in small:
        copy.wait()
    inv_ref[...] = dct_ref[...].T
    for b in range(NZ + 3):
        block = gall[(b % NZ) * TOK:(b % NZ + 1) * TOK, :]
        gown[:, b * TOK:(b + 1) * TOK] = block.T
    pl.semaphore_wait(barrier, NZ + NDP - 2)

    def send_own(q):
        u = place(q)
        @pl.when(u <= 2)
        def _():
            raw(q, u, 0, own=True).start()

        @pl.when(u >= 1)
        def _():
            raw(q, u, 1, own=True).start()

    def send_grads():
        for c in range(2):
            for p in range(4):
                for end in range(2):
                    grads(end, c, p).start()

    def forward1(q):
        u = place(q)

        @pl.when((u == 1) | (u == 2))
        def _():
            raw(q, u - 1, 0).wait_recv()
            raw(q, u - 1, 0).start()
            raw(q, u + 1, 1).wait_recv()
            raw(q, u + 1, 1).start()

    def forward2(q):
        u = place(q)

        @pl.when(u == 2)
        def _():
            raw(q, 0, 0).wait_recv()
            raw(q, 0, 0).start()

        @pl.when(u == 1)
        def _():
            raw(q, 3, 1).wait_recv()
            raw(q, 3, 1).start()

    def make_sums(q):
        u = place(q)
        @pl.when((u == 0) | (u == 3))
        def _():
            for p in range(4):
                @pl.when(u != p)
                def _():
                    raw(q, p, 0).wait_recv()
            end = lax.div(u, 3)
            far = jnp.dot(
                gsum[end], abuf[q].reshape(4 * TOK, CHUNK), preferred_element_type=jnp.float32
            )
            for c in range(2):
                part = far[c * COLS:(c + 1) * COLS]
                top = jnp.maximum(jnp.max(jnp.abs(part), axis=0, keepdims=True), 1e-30)
                sout[q, c] = jnp.round(part * (32767.0 / top)).astype(jnp.int32).astype(jnp.int16)
                unit = top * (1.0 / 32767.0)
                for i in range(TPC):
                    scout[q, c * TPC + i:c * TPC + i + 1, :] = unit[:, i * 128:(i + 1) * 128]
            for copy in sums(q, lax.rem(z + NZ - 1 + 2 * end, NZ)):
                copy.start()

    def pass_sums(q):
        u = place(q)

        @pl.when((u == 0) | (u == 3))
        def _():
            end = lax.div(u, 3)
            for copy in sums(q, right):
                copy.wait_recv()
            for copy in passed(q, lax.rem(z + 1 + (NZ - 2) * end, NZ)):
                copy.start()

    def finish(q):
        u = place(q)
        inner = jnp.where((u == 1) | (u == 2), 1, 0)

        @pl.when(inner == 1)
        def _():
            for copy in passed(q, right):
                copy.wait_recv()

        first = lax.rem(z - u + NZ, NZ)
        near = jnp.dot(
            gown[:, pl.ds(pl.multiple_of(first * TOK, TOK), 4 * TOK)],
            abuf[q].reshape(4 * TOK, CHUNK),
            preferred_element_type=jnp.float32,
        )
        unit = jnp.concatenate(
            [scin[q, pl.ds(inner * TPC + i, 1), :] for i in range(TPC)], axis=1
        )
        accumulated = 0.9 * mbuf[cols(q), :].T + (near + sbuf[q, inner].astype(jnp.float32) * unit)
        coeffs = jnp.dot(
            dct_ref[...], accumulated, precision=HIGH, preferred_element_type=jnp.float32
        )
        lanes = lax.broadcasted_iota(jnp.int32, (64, CHUNK), 0)
        kept = []
        for b in range(2):
            block = coeffs[b * 64:(b + 1) * 64]
            tile_b = jnp.zeros((64, CHUNK), jnp.float32)
            for j in range(4):
                where = pos_ref[b, j:j + 1, cols(q)]
                value = jnp.where(where == lanes, block, 0.0)
                tile_b = tile_b + value
                total = jnp.sum(value, axis=0, keepdims=True)
                spot = where.astype(jnp.float32)
                row = b * 4 + j
                for i in range(TPC):
                    part = slice(i * 128, (i + 1) * 128)
                    msg[q * TPC + i, row:row + 1, :] = total[:, part]
                    msg[q * TPC + i, row + 8:row + 9, :] = spot[:, part]
            kept.append(tile_b)

        def hand_over(i, _):
            t = q * TPC + i

            @pl.when(owner(t) == me)
            def _():
                rx[lax.div(t, NDP), me] = msg[t]

            @pl.when(owner(t) != me)
            def _():
                picks(t, me, owner(t)).start()

            return 0

        lax.fori_loop(0, TPC, hand_over, 0)
        restored = jnp.dot(
            inv_ref[...], jnp.concatenate(kept, axis=0), precision=HIGH,
            preferred_element_type=jnp.float32,
        )
        nmbuf[q] = (accumulated - restored).T
        mom_out(q).start()

    def own1(t):
        @pl.when(owner(t) == me)
        def _():
            slot = lax.div(t, NDP)

            arrived(rx.at[slot, pl.ds(0, NDP - 1)], rx_rs.at[slot])
            lanes = lax.broadcasted_iota(jnp.int32, (64, 128), 0).astype(jnp.float32)

            def add(s, totals):
                m = rx[slot, s]
                out = []
                for b in range(2):
                    total = totals[b]
                    for j in range(4):
                        row = b * 4 + j
                        total = total + jnp.where(
                            m[row + 8:row + 9] == lanes, m[row:row + 1], 0.0
                        )
                    out.append(total)
                return tuple(out)

            zero = jnp.zeros((64, 128), jnp.float32)
            summed = jnp.concatenate(
                lax.fori_loop(0, NDP, add, (zero, zero), unroll=4), axis=0
            )
            sqs[slot, z] = jnp.broadcast_to(
                jnp.sum(summed * summed, axis=0, keepdims=True), (8, 128)
            )

            def tell(d, _):
                squares(slot, z, lax.rem(z + d, NZ)).start()
                return 0

            lax.fori_loop(1, NZ, tell, 0)
            dec[slot] = jnp.dot(
                inv_ref[...], summed, precision=HIGH, preferred_element_type=jnp.float32
            )

    def own2(t):
        @pl.when(owner(t) == me)
        def _():
            slot = lax.div(t, NDP)

            arrived(sqs.at[slot, pl.ds(0, NZ - 1)], sq_rs.at[slot])
            total = sqs[slot, 0, 0:1]
            for s in range(1, NZ):
                total = total + sqs[slot, s, 0:1]
            scale = jnp.sqrt(total * (1.0 / (COLS * NZ)) + 1e-05)
            ust[slot] = (dec[slot] / scale).T.astype(jnp.bfloat16)
            keep(t).start()

            def give(d, _):
                spread(t, lax.rem(me + 2 * d, NDP)).start()
                return 0

            lax.fori_loop(1, NDP // 2, give, 0)
            spread(t, twin).start()

    def relay(t):
        @pl.when((owner(t) != me) & (lax.rem(owner(t), 2) == lax.rem(me, 2)))
        def _():
            onward(t).wait_recv()
            onward(t).start()

    def step(t, _):
        def stage(at, act):
            @pl.when((t >= at) & (t < at + NQ))
            def _():
                act(t - at)

        def tiles(act):
            def run(q):
                def one(i, _):
                    act(q * TPC + i)
                    return 0
                lax.fori_loop(0, TPC, one, 0)
            return run

        stage(AT_FWD1, forward1)
        stage(AT_FWD2, forward2)
        stage(AT_PASS, pass_sums)
        stage(0, send_own)

        @pl.when(t == 0)
        def _():
            send_grads()

        @pl.when(t == AT_SUM)
        def _():
            arrived(gnear, g_rs)
            every = abuf.at[pl.ds(0, NQ // 4)]
            pltpu.make_async_copy(every, every, loc_sem).wait()
            for end in range(2):
                for c in range(2):
                    for p in range(4):
                        gsum[end, c * COLS:(c + 1) * COLS, p * TOK:(p + 1) * TOK] = (
                            gnear[end, c, p].T
                        )

        @pl.when(t == AT_FINISH)
        def _():
            mom_in.wait()

        stage(AT_SUM, make_sums)
        stage(AT_FINISH, finish)
        stage(AT_OWN1, tiles(own1))
        stage(AT_OWN2, tiles(own2))
        stage(AT_RELAY, tiles(relay))
        return 0

    lax.fori_loop(0, NQ + AT_RELAY, step, 0)

    pltpu.make_async_copy(nm_ref, nm_ref, nm_sem).wait()
    sent(gnear, g_ss)
    sent(abuf.at[pl.ds(0, 3 * NQ // 4)], raw_ss)
    sent(sout.at[pl.ds(0, NQ // 2)], sum_ss.at[0])
    sent(scout.at[pl.ds(0, NQ // 2)], sum_ss.at[1])
    sent(sbuf.at[pl.ds(0, NQ // 4)], pass_ss.at[0])
    sent(scin.at[pl.ds(0, NQ // 2)], pass_ss.at[1])

    def drain_tile(t, mine):
        @pl.when(owner(t) == me)
        def _():
            slot = lax.div(t, NDP)
            keep(t).wait()
            sent(sqs.at[slot, pl.ds(0, NZ - 1)], sq_ss.at[slot])
            sent(upd_ref.at[pl.ds(0, NDP // 2 * 128)], up_ss.at[slot])

        @pl.when(lax.rem(owner(t), 2) != lax.rem(me, 2))
        def _():
            onward(t).wait_recv()

        return mine + jnp.where(owner(t) == me, 1, 0)

    mine = lax.fori_loop(0, NT, drain_tile, 0)
    for n in (NT // NDP, SLOTS):
        @pl.when(mine == n)
        def _():
            sent(msg.at[pl.ds(0, NT - n)], msg_ss)
            sent(upd_ref.at[pl.ds(0, (NT // 2 - n) * 128)], relay_ss)


def body(momentum, activations, out_grads, positions):
    hbm = pl.BlockSpec(memory_space=pltpu.HBM)
    dma = pltpu.SemaphoreType.DMA
    new_momentum, update = pl.pallas_call(
        kernel,
        out_shape=(
            jax.ShapeDtypeStruct((ROWS, COLS), jnp.float32),
            jax.ShapeDtypeStruct((ROWS, COLS), jnp.bfloat16),
        ),
        in_specs=[hbm] * 5,
        out_specs=(hbm, hbm),
        scratch_shapes=[
            pltpu.VMEM((NZ * TOK, COLS), jnp.bfloat16),
            pltpu.VMEM((2, 4, ROWS), jnp.int32),
            pltpu.VMEM((COLS, COLS), jnp.float32),
            pltpu.VMEM((COLS, COLS), jnp.float32),
            pltpu.VMEM((NQ, 4, TOK, CHUNK), jnp.bfloat16),
            pltpu.VMEM((COLS, (NZ + 3) * TOK), jnp.bfloat16),
            pltpu.VMEM((2, 2, 4, TOK, COLS), jnp.bfloat16),
            pltpu.VMEM((2, 2 * COLS, 4 * TOK), jnp.bfloat16),
            pltpu.VMEM((ROWS, COLS), jnp.float32),
            pltpu.VMEM((NQ, CHUNK, COLS), jnp.float32),
            pltpu.VMEM((NQ, 2, COLS, CHUNK), jnp.int16),
            pltpu.VMEM((NQ, 8, 128), jnp.float32),
            pltpu.VMEM((NQ, 2, COLS, CHUNK), jnp.int16),
            pltpu.VMEM((NQ, 8, 128), jnp.float32),
            pltpu.VMEM((NT, 16, 128), jnp.float32),
            pltpu.VMEM((SLOTS, NDP, 16, 128), jnp.float32),
            pltpu.VMEM((SLOTS, COLS, 128), jnp.float32),
            pltpu.VMEM((SLOTS, NZ, 8, 128), jnp.float32),
            pltpu.VMEM((SLOTS, 128, COLS), jnp.bfloat16),
            dma, dma, dma, dma, dma((NQ, 4)),
            dma, dma,
            dma((2,)), dma((NQ, 2)), dma((2,)),
            dma, dma((SLOTS,)),
            dma((SLOTS,)), dma((SLOTS,)),
            dma((SLOTS,)), dma((NT,)), dma((SLOTS,)), dma, dma((3,)),
        ],
        compiler_params=pltpu.CompilerParams(
            collective_id=0, has_side_effects=True, vmem_limit_bytes=60 << 20
        ),
    )(activations, momentum[0], out_grads, positions[0], dct_blocks())
    return new_momentum[None], update


def solution(mesh):
    placed = (
        P("dp", None, "tensor"),
        P(("dp", "tensor"), None),
        P("dp", "tensor"),
        P("dp", "tensor", None, None),
    )
    return jax.shard_map(
        body,
        mesh=mesh,
        in_specs=placed,
        out_specs=(P("dp", None, "tensor"), P(None, "tensor")),
        check_vma=False,
    )
```

```python
import functools

import jax
import jax.numpy as jnp
import numpy as np
from jax import lax
from jax.experimental import pallas as pl
from jax.experimental.pallas import tpu as pltpu
from jax.sharding import PartitionSpec as P

MESH = pl.DeviceIdType.MESH
ROWS, COLS, TOK = 5120, 128, 128
NZ, NDP = 8, 32
CHUNK = 256
NQ = ROWS // CHUNK
TPC = CHUNK // 128
NT = ROWS // 128
SLOTS = -(-NT // NDP)

AT_FWD1, AT_FWD2, AT_SUM, AT_PASS, AT_FINISH = 3, 6, 8, 11, 13
AT_OWN1, AT_OWN2, AT_RELAY = 16, 21, 27


def dct_blocks():
    freq = np.arange(64, dtype=np.float64)[:, None]
    place = np.arange(64, dtype=np.float64)[None, :]
    scales = np.where(freq == 0, 1.0 / 8.0, np.sqrt(2.0 / 64.0))
    table = scales * np.cos(np.pi * (2.0 * place + 1.0) * freq / 128.0)
    blocks = np.kron(np.eye(COLS // 64), table)
    high = blocks.astype(jnp.bfloat16)
    low = (blocks - high.astype(np.float64)).astype(jnp.bfloat16)
    return np.stack([
        np.concatenate([high, high, low], axis=1),
        np.concatenate([high.T, high.T, low.T], axis=1),
    ])


def product(parts, x):
    high = x.astype(jnp.bfloat16)
    low = (x - high.astype(jnp.float32)).astype(jnp.bfloat16)
    return jnp.dot(
        parts, jnp.concatenate([high, low, high], axis=0), preferred_element_type=jnp.float32
    )


def kernel(
    a_ref, m_ref, g_ref, pos_hbm, dct_hbm,
    nm_ref, upd_ref,
    gall, pos_ref, dct_ref,
    abuf, gown, gnear, gsum, mbuf, nmbuf, sout, scout, sbuf, scin,
    msg, rx, dec, sqs, uall,
    loc_sem, m_sem, nm_sem, raw_ss, raw_rs, g_ss, g_rs,
    sum_ss, sum_rs, pass_ss, msg_ss, rx_rs, sq_ss, sq_rs, up_ss, up_rs, ul_sem, relay_ss, in_sem,
):
    me = lax.axis_index("dp")
    z = lax.axis_index("tensor")
    right = lax.rem(z + 1, NZ)
    left = lax.rem(z + NZ - 1, NZ)
    twin = me + 1 - 2 * lax.rem(me, 2)

    def place(q):
        return lax.rem(z + 4 - lax.rem(q, 4), 4)

    def cols(q):
        return pl.ds(pl.multiple_of(q * CHUNK, CHUNK), CHUNK)

    def owner(t):
        return lax.rem(t * 5, NDP)

    mom_in = pltpu.make_async_copy(m_ref, mbuf, m_sem)

    def mom_out(q):
        return pltpu.make_async_copy(nmbuf.at[q], nm_ref.at[cols(q)], nm_sem)

    def own_local(q):
        return pltpu.make_async_copy(a_ref.at[:, cols(q)], abuf.at[q, place(q)], loc_sem)

    def sent(ref, sem):
        pltpu.make_async_remote_copy(
            src_ref=ref, dst_ref=ref, send_sem=sem, recv_sem=sem,
            device_id={"tensor": right}, device_id_type=MESH,
        ).wait_send()

    def arrived(ref, sem):
        pltpu.make_async_remote_copy(
            src_ref=ref, dst_ref=ref, send_sem=sem, recv_sem=sem,
            device_id={"tensor": right}, device_id_type=MESH,
        ).wait_recv()

    def raw(q, p, way):
        return pltpu.make_async_remote_copy(
            src_ref=abuf.at[q, p],
            dst_ref=abuf.at[q, p],
            send_sem=raw_ss,
            recv_sem=raw_rs.at[q, p],
            device_id={"tensor": left if way else right},
            device_id_type=MESH,
        )

    def grads(end, c, p):
        target = lax.rem(z + (NZ - 1 - c if end else 1 + c), NZ)
        block = lax.rem(target + (NZ - 3 if end else 0) + p, NZ)
        return pltpu.make_async_remote_copy(
            src_ref=g_ref.at[pl.ds(pl.multiple_of(block * TOK, TOK), TOK)],
            dst_ref=gnear.at[end, c, p],
            send_sem=g_ss,
            recv_sem=g_rs,
            device_id={"tensor": target},
            device_id_type=MESH,
        )

    def sums(q, target):
        return (
            pltpu.make_async_remote_copy(
                src_ref=sout.at[q], dst_ref=sbuf.at[q],
                send_sem=sum_ss.at[0], recv_sem=sum_rs.at[q, 0],
                device_id={"tensor": target}, device_id_type=MESH,
            ),
            pltpu.make_async_remote_copy(
                src_ref=scout.at[q], dst_ref=scin.at[q],
                send_sem=sum_ss.at[1], recv_sem=sum_rs.at[q, 1],
                device_id={"tensor": target}, device_id_type=MESH,
            ),
        )

    def passed(q, target):
        return (
            pltpu.make_async_remote_copy(
                src_ref=sbuf.at[q, 1], dst_ref=sbuf.at[q, 1],
                send_sem=pass_ss.at[0], recv_sem=sum_rs.at[q, 0],
                device_id={"tensor": target}, device_id_type=MESH,
            ),
            pltpu.make_async_remote_copy(
                src_ref=scin.at[q], dst_ref=scin.at[q],
                send_sem=pass_ss.at[1], recv_sem=sum_rs.at[q, 1],
                device_id={"tensor": target}, device_id_type=MESH,
            ),
        )

    def picks(t, source, target):
        slot = lax.div(t, NDP)
        return pltpu.make_async_remote_copy(
            src_ref=msg.at[t], dst_ref=rx.at[slot, source],
            send_sem=msg_ss, recv_sem=rx_rs.at[slot],
            device_id={"dp": target}, device_id_type=MESH,
        )

    def squares(slot, source, target):
        return pltpu.make_async_remote_copy(
            src_ref=sqs.at[slot, z], dst_ref=sqs.at[slot, source],
            send_sem=sq_ss.at[slot], recv_sem=sq_rs.at[slot],
            device_id={"tensor": target}, device_id_type=MESH,
        )

    def tile(t):
        return pl.ds(pl.multiple_of(t * 128, 128), 128)

    def spread(t, target):
        slot = lax.div(t, NDP)
        return pltpu.make_async_remote_copy(
            src_ref=uall.at[tile(t)], dst_ref=uall.at[tile(t)],
            send_sem=up_ss.at[slot], recv_sem=up_rs.at[t],
            device_id={"dp": target}, device_id_type=MESH,
        )

    def onward(t):
        return pltpu.make_async_remote_copy(
            src_ref=uall.at[tile(t)], dst_ref=uall.at[tile(t)],
            send_sem=relay_ss, recv_sem=up_rs.at[t],
            device_id={"dp": twin}, device_id_type=MESH,
        )

    def start_own(q, _):
        own_local(q).start()
        return 0

    small = [
        pltpu.make_async_copy(source, target, in_sem.at[i])
        for i, (source, target) in enumerate(
            ((g_ref, gall), (pos_hbm, pos_ref), (dct_hbm, dct_ref))
        )
    ]
    for copy in small:
        copy.start()
    mom_in.start()
    lax.fori_loop(0, NQ, start_own, 0)
    barrier = pltpu.get_barrier_semaphore()

    def greet_z(d, _):
        pl.semaphore_signal(
            barrier, inc=1, device_id={"tensor": lax.rem(z + d, NZ)}, device_id_type=MESH
        )
        return 0

    def greet_dp(d, _):
        pl.semaphore_signal(
            barrier, inc=1, device_id={"dp": lax.rem(me + d, NDP)}, device_id_type=MESH
        )
        return 0

    lax.fori_loop(1, NZ, greet_z, 0)
    lax.fori_loop(1, NDP, greet_dp, 0)
    for copy in small:
        copy.wait()
    for b in range(NZ + 3):
        block = gall[(b % NZ) * TOK:(b % NZ + 1) * TOK, :]
        gown[:, b * TOK:(b + 1) * TOK] = block.T
    every = abuf.at[pl.ds(0, NQ // 4)]
    pltpu.make_async_copy(every, every, loc_sem).wait()
    pl.semaphore_wait(barrier, NZ + NDP - 2)

    def send_own(q):
        u = place(q)
        @pl.when(u <= 2)
        def _():
            raw(q, u, 0).start()

        @pl.when(u >= 1)
        def _():
            raw(q, u, 1).start()

    def send_grads():
        for c in range(2):
            for p in range(4):
                for end in range(2):
                    grads(end, c, p).start()

    def forward1(q):
        u = place(q)

        @pl.when((u == 1) | (u == 2))
        def _():
            raw(q, u - 1, 0).wait_recv()
            raw(q, u - 1, 0).start()
            raw(q, u + 1, 1).wait_recv()
            raw(q, u + 1, 1).start()

    def forward2(q):
        u = place(q)

        @pl.when(u == 2)
        def _():
            raw(q, 0, 0).wait_recv()
            raw(q, 0, 0).start()

        @pl.when(u == 1)
        def _():
            raw(q, 3, 1).wait_recv()
            raw(q, 3, 1).start()

    def make_sums(q):
        u = place(q)
        @pl.when((u == 0) | (u == 3))
        def _():
            for p in range(4):
                @pl.when(u != p)
                def _():
                    raw(q, p, 0).wait_recv()
            end = lax.div(u, 3)
            far = jnp.dot(
                gsum[end], abuf[q].reshape(4 * TOK, CHUNK), preferred_element_type=jnp.float32
            )
            for c in range(2):
                part = far[c * COLS:(c + 1) * COLS]
                top = jnp.maximum(jnp.max(jnp.abs(part), axis=0, keepdims=True), 1e-30)
                sout[q, c] = jnp.round(part * (32767.0 / top)).astype(jnp.int32).astype(jnp.int16)
                unit = top * (1.0 / 32767.0)
                for i in range(TPC):
                    scout[q, c * TPC + i:c * TPC + i + 1, :] = unit[:, i * 128:(i + 1) * 128]
            for copy in sums(q, lax.rem(z + NZ - 1 + 2 * end, NZ)):
                copy.start()

    def pass_sums(q):
        u = place(q)

        @pl.when((u == 0) | (u == 3))
        def _():
            end = lax.div(u, 3)
            for copy in sums(q, right):
                copy.wait_recv()
            for copy in passed(q, lax.rem(z + 1 + (NZ - 2) * end, NZ)):
                copy.start()

    def finish(q):
        u = place(q)
        inner = jnp.where((u == 1) | (u == 2), 1, 0)

        @pl.when(inner == 1)
        def _():
            for copy in passed(q, right):
                copy.wait_recv()

        first = lax.rem(z - u + NZ, NZ)
        near = jnp.dot(
            gown[:, pl.ds(pl.multiple_of(first * TOK, TOK), 4 * TOK)],
            abuf[q].reshape(4 * TOK, CHUNK),
            preferred_element_type=jnp.float32,
        )
        unit = jnp.concatenate(
            [scin[q, pl.ds(inner * TPC + i, 1), :] for i in range(TPC)], axis=1
        )
        accumulated = 0.9 * mbuf[cols(q), :].T + (near + sbuf[q, inner].astype(jnp.float32) * unit)
        coeffs = product(dct_ref[0], accumulated)
        lanes = lax.broadcasted_iota(jnp.int32, (64, CHUNK), 0)
        kept = []
        for b in range(2):
            block = coeffs[b * 64:(b + 1) * 64]
            tile_b = jnp.zeros((64, CHUNK), jnp.float32)
            for j in range(4):
                where = pos_ref[b, j:j + 1, cols(q)]
                value = jnp.where(where == lanes, block, 0.0)
                tile_b = tile_b + value
                total = jnp.sum(value, axis=0, keepdims=True)
                spot = where.astype(jnp.float32)
                row = b * 4 + j
                for i in range(TPC):
                    part = slice(i * 128, (i + 1) * 128)
                    msg[q * TPC + i, row:row + 1, :] = total[:, part]
                    msg[q * TPC + i, row + 8:row + 9, :] = spot[:, part]
            kept.append(tile_b)

        def hand_over(i, _):
            t = q * TPC + i

            @pl.when(owner(t) == me)
            def _():
                rx[lax.div(t, NDP), me] = msg[t]

            @pl.when(owner(t) != me)
            def _():
                picks(t, me, owner(t)).start()

            return 0

        lax.fori_loop(0, TPC, hand_over, 0)
        restored = product(dct_ref[1], jnp.concatenate(kept, axis=0))
        nmbuf[q] = (accumulated - restored).T
        mom_out(q).start()

    def own1(t):
        @pl.when(owner(t) == me)
        def _():
            slot = lax.div(t, NDP)

            arrived(rx.at[slot, pl.ds(0, NDP - 1)], rx_rs.at[slot])
            lanes = lax.broadcasted_iota(jnp.int32, (64, 128), 0).astype(jnp.float32)

            def add(s, totals):
                m = rx[slot, s]
                out = []
                for b in range(2):
                    total = totals[b]
                    for j in range(4):
                        row = b * 4 + j
                        total = total + jnp.where(
                            m[row + 8:row + 9] == lanes, m[row:row + 1], 0.0
                        )
                    out.append(total)
                return tuple(out)

            zero = jnp.zeros((64, 128), jnp.float32)
            summed = jnp.concatenate(
                lax.fori_loop(0, NDP, add, (zero, zero), unroll=4), axis=0
            )
            sqs[slot, z] = jnp.broadcast_to(
                jnp.sum(summed * summed, axis=0, keepdims=True), (8, 128)
            )

            def tell(d, _):
                squares(slot, z, lax.rem(z + d, NZ)).start()
                return 0

            lax.fori_loop(1, NZ, tell, 0)
            dec[slot] = product(dct_ref[1], summed)

    def own2(t):
        @pl.when(owner(t) == me)
        def _():
            slot = lax.div(t, NDP)

            arrived(sqs.at[slot, pl.ds(0, NZ - 1)], sq_rs.at[slot])
            total = sqs[slot, 0, 0:1]
            for s in range(1, NZ):
                total = total + sqs[slot, s, 0:1]
            scale = jnp.sqrt(total * (1.0 / (COLS * NZ)) + 1e-05)
            uall[tile(t), :] = (dec[slot] / scale).T.astype(jnp.bfloat16)

            def give(d, _):
                spread(t, lax.rem(me + 2 * d, NDP)).start()
                return 0

            lax.fori_loop(1, NDP // 2, give, 0)
            spread(t, twin).start()

    def relay(t):
        @pl.when((owner(t) != me) & (lax.rem(owner(t), 2) == lax.rem(me, 2)))
        def _():
            onward(t).wait_recv()
            onward(t).start()

    def step(t, _):
        def stage(at, act):
            @pl.when((t >= at) & (t < at + NQ))
            def _():
                act(t - at)

        def tiles(act):
            def run(q):
                def one(i, _):
                    act(q * TPC + i)
                    return 0
                lax.fori_loop(0, TPC, one, 0)
            return run

        stage(AT_FWD1, forward1)
        stage(AT_FWD2, forward2)
        stage(AT_PASS, pass_sums)
        stage(0, send_own)

        @pl.when(t == 0)
        def _():
            send_grads()

        @pl.when(t == AT_SUM)
        def _():
            arrived(gnear, g_rs)
            for end in range(2):
                for c in range(2):
                    for p in range(4):
                        gsum[end, c * COLS:(c + 1) * COLS, p * TOK:(p + 1) * TOK] = (
                            gnear[end, c, p].T
                        )

        @pl.when(t == AT_FINISH)
        def _():
            mom_in.wait()

        stage(AT_SUM, make_sums)
        stage(AT_FINISH, finish)
        stage(AT_OWN1, tiles(own1))
        stage(AT_OWN2, tiles(own2))
        stage(AT_RELAY, tiles(relay))
        return 0

    lax.fori_loop(0, NQ + AT_RELAY, step, 0)

    pltpu.make_async_copy(nm_ref, nm_ref, nm_sem).wait()
    sent(gnear, g_ss)
    sent(abuf.at[pl.ds(0, 3 * NQ // 4)], raw_ss)
    sent(sout.at[pl.ds(0, NQ // 2)], sum_ss.at[0])
    sent(scout.at[pl.ds(0, NQ // 2)], sum_ss.at[1])
    sent(sbuf.at[pl.ds(0, NQ // 4)], pass_ss.at[0])
    sent(scin.at[pl.ds(0, NQ // 2)], pass_ss.at[1])

    def drain_tile(t, mine):
        @pl.when(owner(t) == me)
        def _():
            slot = lax.div(t, NDP)
            sent(sqs.at[slot, pl.ds(0, NZ - 1)], sq_ss.at[slot])
            sent(uall.at[pl.ds(0, NDP // 2 * 128)], up_ss.at[slot])

        @pl.when(lax.rem(owner(t), 2) != lax.rem(me, 2))
        def _():
            onward(t).wait_recv()

        return mine + jnp.where(owner(t) == me, 1, 0)

    mine = lax.fori_loop(0, NT, drain_tile, 0)
    whole = pltpu.make_async_copy(uall, upd_ref, ul_sem)
    whole.start()
    for n in (NT // NDP, SLOTS):
        @pl.when(mine == n)
        def _():
            sent(msg.at[pl.ds(0, NT - n)], msg_ss)
            sent(uall.at[pl.ds(0, (NT // 2 - n) * 128)], relay_ss)

    whole.wait()


def hand_out(nm_in, upd_in, nm_out, upd_out, nm_mid, upd_mid, sem):
    parts = [pl.ds(k * ROWS // 8, ROWS // 8) for k in range(8)]
    triples = [(nm_in, nm_mid, nm_out), (upd_in, upd_mid, upd_out)]

    def copy(i, j, way):
        return pltpu.make_async_copy(
            triples[i][way].at[parts[j]], triples[i][way + 1].at[parts[j]], sem.at[way, i, j]
        )

    every = [(i, j) for j in range(8) for i in range(2)]
    for i, j in every:
        copy(i, j, 0).start()
    for i, j in every:
        copy(i, j, 0).wait()
        copy(i, j, 1).start()
    for i, j in every:
        copy(i, j, 1).wait()


def body(momentum, activations, out_grads, positions):
    hbm = pl.BlockSpec(memory_space=pltpu.HBM)
    dma = pltpu.SemaphoreType.DMA
    new_momentum, update = pl.pallas_call(
        kernel,
        out_shape=(
            jax.ShapeDtypeStruct((ROWS, COLS), jnp.float32),
            jax.ShapeDtypeStruct((ROWS, COLS), jnp.bfloat16),
        ),
        in_specs=[hbm] * 5,
        out_specs=(hbm, hbm),
        scratch_shapes=[
            pltpu.VMEM((NZ * TOK, COLS), jnp.bfloat16),
            pltpu.VMEM((2, 4, ROWS), jnp.int32),
            pltpu.VMEM((2, COLS, 3 * COLS), jnp.bfloat16),
            pltpu.VMEM((NQ, 4, TOK, CHUNK), jnp.bfloat16),
            pltpu.VMEM((COLS, (NZ + 3) * TOK), jnp.bfloat16),
            pltpu.VMEM((2, 2, 4, TOK, COLS), jnp.bfloat16),
            pltpu.VMEM((2, 2 * COLS, 4 * TOK), jnp.bfloat16),
            pltpu.VMEM((ROWS, COLS), jnp.float32),
            pltpu.VMEM((NQ, CHUNK, COLS), jnp.float32),
            pltpu.VMEM((NQ, 2, COLS, CHUNK), jnp.int16),
            pltpu.VMEM((NQ, 8, 128), jnp.float32),
            pltpu.VMEM((NQ, 2, COLS, CHUNK), jnp.int16),
            pltpu.VMEM((NQ, 8, 128), jnp.float32),
            pltpu.VMEM((NT, 16, 128), jnp.float32),
            pltpu.VMEM((SLOTS, NDP, 16, 128), jnp.float32),
            pltpu.VMEM((SLOTS, COLS, 128), jnp.float32),
            pltpu.VMEM((SLOTS, NZ, 8, 128), jnp.float32),
            pltpu.VMEM((ROWS, COLS), jnp.bfloat16),
            dma, dma, dma, dma, dma((NQ, 4)),
            dma, dma,
            dma((2,)), dma((NQ, 2)), dma((2,)),
            dma, dma((SLOTS,)),
            dma((SLOTS,)), dma((SLOTS,)),
            dma((SLOTS,)), dma((NT,)), dma, dma, dma((3,)),
        ],
        compiler_params=pltpu.CompilerParams(
            collective_id=0, has_side_effects=True, vmem_limit_bytes=60 << 20
        ),
    )(activations, momentum[0], out_grads, positions[0], dct_blocks())
    shapes = (
        jax.ShapeDtypeStruct((ROWS, COLS), jnp.float32),
        jax.ShapeDtypeStruct((ROWS, COLS), jnp.bfloat16),
    )
    new_momentum, update = pl.pallas_call(
        hand_out,
        out_shape=shapes,
        in_specs=[hbm] * 2,
        out_specs=(hbm, hbm),
        scratch_shapes=[pltpu.VMEM(s.shape, s.dtype) for s in shapes] + [dma((2, 2, 8))],
        compiler_params=pltpu.CompilerParams(vmem_limit_bytes=62 << 20),
    )(new_momentum, update)
    return new_momentum[None], update


def solution(mesh):
    placed = (
        P("dp", None, "tensor"),
        P(("dp", "tensor"), None),
        P("dp", "tensor"),
        P("dp", "tensor", None, None),
    )
    return jax.shard_map(
        body,
        mesh=mesh,
        in_specs=placed,
        out_specs=(P("dp", None, "tensor"), P(None, "tensor")),
        check_vma=False,
    )
```

```python
import functools

import jax
import jax.numpy as jnp
import numpy as np
from jax import lax
from jax.experimental import pallas as pl
from jax.experimental.pallas import tpu as pltpu
from jax.sharding import PartitionSpec as P

MESH = pl.DeviceIdType.MESH
ROWS, COLS, TOK = 5120, 128, 128
NZ, NDP = 8, 32
CHUNK = 256
NQ = ROWS // CHUNK
TPC = CHUNK // 128
NT = ROWS // 128
SLOTS = -(-NT // NDP)

AT_FWD1, AT_FWD2, AT_SUM, AT_PASS, AT_FINISH = 3, 5, 7, 9, 11
AT_OWN1, AT_OWN2, AT_RELAY = 14, 19, 25


def dct_blocks():
    freq = np.arange(64, dtype=np.float64)[:, None]
    place = np.arange(64, dtype=np.float64)[None, :]
    scales = np.where(freq == 0, 1.0 / 8.0, np.sqrt(2.0 / 64.0))
    table = scales * np.cos(np.pi * (2.0 * place + 1.0) * freq / 128.0)
    blocks = np.kron(np.eye(COLS // 64), table)
    high = blocks.astype(jnp.bfloat16)
    low = (blocks - high.astype(np.float64)).astype(jnp.bfloat16)
    return np.stack([
        np.concatenate([high, high, low], axis=1),
        np.concatenate([high.T, high.T, low.T], axis=1),
    ])


def product(parts, x):
    high = x.astype(jnp.bfloat16)
    low = (x - high.astype(jnp.float32)).astype(jnp.bfloat16)
    return jnp.dot(
        parts, jnp.concatenate([high, low, high], axis=0), preferred_element_type=jnp.float32
    )


def kernel(
    a_ref, m_ref, g_ref, pos_hbm, dct_hbm,
    nm_ref, upd_ref,
    gall, pos_ref, dct_ref,
    abuf, gown, gnear, gsum, mbuf, nmbuf, sout, scout, sbuf, scin,
    msg, rx, dec, sqs, uall,
    loc_sem, m_sem, nm_sem, raw_ss, raw_rs, g_ss, g_rs,
    sum_ss, sum_rs, pass_ss, msg_ss, rx_rs, sq_ss, sq_rs, up_ss, up_rs, ul_sem, relay_ss, in_sem,
):
    me = lax.axis_index("dp")
    z = lax.axis_index("tensor")
    right = lax.rem(z + 1, NZ)
    left = lax.rem(z + NZ - 1, NZ)
    twin = me + 1 - 2 * lax.rem(me, 2)

    def place(q):
        return lax.rem(z + 4 - lax.rem(q, 4), 4)

    def cols(q):
        return pl.ds(pl.multiple_of(q * CHUNK, CHUNK), CHUNK)

    def owner(t):
        return lax.rem(t * 5, NDP)

    mom_in = pltpu.make_async_copy(m_ref, mbuf, m_sem)

    def mom_out(q):
        return pltpu.make_async_copy(nmbuf.at[q], nm_ref.at[cols(q)], nm_sem)

    def own_local(q):
        return pltpu.make_async_copy(a_ref.at[:, cols(q)], abuf.at[q, place(q)], loc_sem)

    def sent(ref, sem):
        pltpu.make_async_remote_copy(
            src_ref=ref, dst_ref=ref, send_sem=sem, recv_sem=sem,
            device_id={"tensor": right}, device_id_type=MESH,
        ).wait_send()

    def arrived(ref, sem):
        pltpu.make_async_remote_copy(
            src_ref=ref, dst_ref=ref, send_sem=sem, recv_sem=sem,
            device_id={"tensor": right}, device_id_type=MESH,
        ).wait_recv()

    def raw(q, p, way):
        return pltpu.make_async_remote_copy(
            src_ref=abuf.at[q, p],
            dst_ref=abuf.at[q, p],
            send_sem=raw_ss,
            recv_sem=raw_rs.at[q, p],
            device_id={"tensor": left if way else right},
            device_id_type=MESH,
        )

    def grads(end, c, p):
        target = lax.rem(z + (NZ - 1 - c if end else 1 + c), NZ)
        block = lax.rem(target + (NZ - 3 if end else 0) + p, NZ)
        return pltpu.make_async_remote_copy(
            src_ref=g_ref.at[pl.ds(pl.multiple_of(block * TOK, TOK), TOK)],
            dst_ref=gnear.at[end, c, p],
            send_sem=g_ss,
            recv_sem=g_rs,
            device_id={"tensor": target},
            device_id_type=MESH,
        )

    def sums(q, target):
        return (
            pltpu.make_async_remote_copy(
                src_ref=sout.at[q], dst_ref=sbuf.at[q],
                send_sem=sum_ss.at[0], recv_sem=sum_rs.at[q, 0],
                device_id={"tensor": target}, device_id_type=MESH,
            ),
            pltpu.make_async_remote_copy(
                src_ref=scout.at[q], dst_ref=scin.at[q],
                send_sem=sum_ss.at[1], recv_sem=sum_rs.at[q, 1],
                device_id={"tensor": target}, device_id_type=MESH,
            ),
        )

    def passed(q, target):
        return (
            pltpu.make_async_remote_copy(
                src_ref=sbuf.at[q, 1], dst_ref=sbuf.at[q, 1],
                send_sem=pass_ss.at[0], recv_sem=sum_rs.at[q, 0],
                device_id={"tensor": target}, device_id_type=MESH,
            ),
            pltpu.make_async_remote_copy(
                src_ref=scin.at[q], dst_ref=scin.at[q],
                send_sem=pass_ss.at[1], recv_sem=sum_rs.at[q, 1],
                device_id={"tensor": target}, device_id_type=MESH,
            ),
        )

    def picks(t, source, target):
        slot = lax.div(t, NDP)
        return pltpu.make_async_remote_copy(
            src_ref=msg.at[t], dst_ref=rx.at[slot, source],
            send_sem=msg_ss, recv_sem=rx_rs.at[slot],
            device_id={"dp": target}, device_id_type=MESH,
        )

    def squares(slot, source, target):
        return pltpu.make_async_remote_copy(
            src_ref=sqs.at[slot, z], dst_ref=sqs.at[slot, source],
            send_sem=sq_ss.at[slot], recv_sem=sq_rs.at[slot],
            device_id={"tensor": target}, device_id_type=MESH,
        )

    def tile(t):
        return pl.ds(pl.multiple_of(t * 128, 128), 128)

    def spread(t, target):
        slot = lax.div(t, NDP)
        return pltpu.make_async_remote_copy(
            src_ref=uall.at[tile(t)], dst_ref=uall.at[tile(t)],
            send_sem=up_ss.at[slot], recv_sem=up_rs.at[t],
            device_id={"dp": target}, device_id_type=MESH,
        )

    def onward(t):
        return pltpu.make_async_remote_copy(
            src_ref=uall.at[tile(t)], dst_ref=uall.at[tile(t)],
            send_sem=relay_ss, recv_sem=up_rs.at[t],
            device_id={"dp": twin}, device_id_type=MESH,
        )

    def start_own(q, _):
        own_local(q).start()
        return 0

    small = [
        pltpu.make_async_copy(source, target, in_sem.at[i])
        for i, (source, target) in enumerate(
            ((g_ref, gall), (pos_hbm, pos_ref), (dct_hbm, dct_ref))
        )
    ]
    for copy in small:
        copy.start()
    mom_in.start()
    lax.fori_loop(0, NQ, start_own, 0)
    barrier = pltpu.get_barrier_semaphore()

    def greet_z(d, _):
        pl.semaphore_signal(
            barrier, inc=1, device_id={"tensor": lax.rem(z + d, NZ)}, device_id_type=MESH
        )
        return 0

    def greet_dp(d, _):
        pl.semaphore_signal(
            barrier, inc=1, device_id={"dp": lax.rem(me + d, NDP)}, device_id_type=MESH
        )
        return 0

    lax.fori_loop(1, NZ, greet_z, 0)
    lax.fori_loop(1, NDP, greet_dp, 0)
    for copy in small:
        copy.wait()
    for b in range(NZ + 3):
        block = gall[(b % NZ) * TOK:(b % NZ + 1) * TOK, :]
        gown[:, b * TOK:(b + 1) * TOK] = block.T
    every = abuf.at[pl.ds(0, NQ // 4)]
    pltpu.make_async_copy(every, every, loc_sem).wait()
    pl.semaphore_wait(barrier, NZ + NDP - 2)

    def send_own(q):
        u = place(q)
        @pl.when(u <= 2)
        def _():
            raw(q, u, 0).start()

        @pl.when(u >= 1)
        def _():
            raw(q, u, 1).start()

    def send_grads(p):
        for c in range(2):
            for end in range(2):
                grads(end, c, p).start()

    def forward1(q):
        u = place(q)

        @pl.when((u == 1) | (u == 2))
        def _():
            raw(q, u - 1, 0).wait_recv()
            raw(q, u - 1, 0).start()
            raw(q, u + 1, 1).wait_recv()
            raw(q, u + 1, 1).start()

    def forward2(q):
        u = place(q)

        @pl.when(u == 2)
        def _():
            raw(q, 0, 0).wait_recv()
            raw(q, 0, 0).start()

        @pl.when(u == 1)
        def _():
            raw(q, 3, 1).wait_recv()
            raw(q, 3, 1).start()

    def make_sums(q):
        u = place(q)
        @pl.when((u == 0) | (u == 3))
        def _():
            for p in range(4):
                @pl.when(u != p)
                def _():
                    raw(q, p, 0).wait_recv()
            end = lax.div(u, 3)
            far = jnp.dot(
                gsum[end], abuf[q].reshape(4 * TOK, CHUNK), preferred_element_type=jnp.float32
            )
            for c in range(2):
                part = far[c * COLS:(c + 1) * COLS]
                top = jnp.maximum(jnp.max(jnp.abs(part), axis=0, keepdims=True), 1e-30)
                sout[q, c] = jnp.round(part * (32767.0 / top)).astype(jnp.int32).astype(jnp.int16)
                unit = top * (1.0 / 32767.0)
                for i in range(TPC):
                    scout[q, c * TPC + i:c * TPC + i + 1, :] = unit[:, i * 128:(i + 1) * 128]
            for copy in sums(q, lax.rem(z + NZ - 1 + 2 * end, NZ)):
                copy.start()

    def pass_sums(q):
        u = place(q)

        @pl.when((u == 0) | (u == 3))
        def _():
            end = lax.div(u, 3)
            for copy in sums(q, right):
                copy.wait_recv()
            for copy in passed(q, lax.rem(z + 1 + (NZ - 2) * end, NZ)):
                copy.start()

    def finish(q):
        u = place(q)
        inner = jnp.where((u == 1) | (u == 2), 1, 0)

        @pl.when(inner == 1)
        def _():
            for copy in passed(q, right):
                copy.wait_recv()

        first = lax.rem(z - u + NZ, NZ)
        near = jnp.dot(
            gown[:, pl.ds(pl.multiple_of(first * TOK, TOK), 4 * TOK)],
            abuf[q].reshape(4 * TOK, CHUNK),
            preferred_element_type=jnp.float32,
        )
        unit = jnp.concatenate(
            [scin[q, pl.ds(inner * TPC + i, 1), :] for i in range(TPC)], axis=1
        )
        accumulated = 0.9 * mbuf[cols(q), :].T + (near + sbuf[q, inner].astype(jnp.float32) * unit)
        coeffs = product(dct_ref[0], accumulated)
        lanes = lax.broadcasted_iota(jnp.int32, (64, CHUNK), 0)
        kept = []
        for b in range(2):
            block = coeffs[b * 64:(b + 1) * 64]
            tile_b = jnp.zeros((64, CHUNK), jnp.float32)
            for j in range(4):
                where = pos_ref[b, j:j + 1, cols(q)]
                value = jnp.where(where == lanes, block, 0.0)
                tile_b = tile_b + value
                total = jnp.sum(value, axis=0, keepdims=True)
                spot = where.astype(jnp.float32)
                row = b * 4 + j
                for i in range(TPC):
                    part = slice(i * 128, (i + 1) * 128)
                    msg[q * TPC + i, row:row + 1, :] = total[:, part]
                    msg[q * TPC + i, row + 8:row + 9, :] = spot[:, part]
            kept.append(tile_b)

        def hand_over(i, _):
            t = q * TPC + i

            @pl.when(owner(t) == me)
            def _():
                rx[lax.div(t, NDP), me] = msg[t]

            @pl.when(owner(t) != me)
            def _():
                picks(t, me, owner(t)).start()

            return 0

        lax.fori_loop(0, TPC, hand_over, 0)
        restored = product(dct_ref[1], jnp.concatenate(kept, axis=0))
        nmbuf[q] = (accumulated - restored).T
        mom_out(q).start()

    def own1(t):
        @pl.when(owner(t) == me)
        def _():
            slot = lax.div(t, NDP)

            arrived(rx.at[slot, pl.ds(0, NDP - 1)], rx_rs.at[slot])
            lanes = lax.broadcasted_iota(jnp.int32, (64, 128), 0).astype(jnp.float32)

            def add(s, totals):
                m = rx[slot, s]
                out = []
                for b in range(2):
                    total = totals[b]
                    for j in range(4):
                        row = b * 4 + j
                        total = total + jnp.where(
                            m[row + 8:row + 9] == lanes, m[row:row + 1], 0.0
                        )
                    out.append(total)
                return tuple(out)

            zero = jnp.zeros((64, 128), jnp.float32)
            summed = jnp.concatenate(
                lax.fori_loop(0, NDP, add, (zero, zero), unroll=4), axis=0
            )
            sqs[slot, z] = jnp.broadcast_to(
                jnp.sum(summed * summed, axis=0, keepdims=True), (8, 128)
            )

            def tell(d, _):
                squares(slot, z, lax.rem(z + d, NZ)).start()
                return 0

            lax.fori_loop(1, NZ, tell, 0)
            dec[slot] = product(dct_ref[1], summed)

    def own2(t):
        @pl.when(owner(t) == me)
        def _():
            slot = lax.div(t, NDP)

            arrived(sqs.at[slot, pl.ds(0, NZ - 1)], sq_rs.at[slot])
            total = sqs[slot, 0, 0:1]
            for s in range(1, NZ):
                total = total + sqs[slot, s, 0:1]
            scale = jnp.sqrt(total * (1.0 / (COLS * NZ)) + 1e-05)
            uall[tile(t), :] = (dec[slot] / scale).T.astype(jnp.bfloat16)

            def give(d, _):
                spread(t, lax.rem(me + 2 * d, NDP)).start()
                return 0

            lax.fori_loop(1, NDP // 2, give, 0)
            spread(t, twin).start()

    def relay(t):
        @pl.when((owner(t) != me) & (lax.rem(owner(t), 2) == lax.rem(me, 2)))
        def _():
            onward(t).wait_recv()
            onward(t).start()

    def step(t, _):
        def stage(at, act):
            @pl.when((t >= at) & (t < at + NQ))
            def _():
                act(t - at)

        def tiles(act):
            def run(q):
                def one(i, _):
                    act(q * TPC + i)
                    return 0
                lax.fori_loop(0, TPC, one, 0)
            return run

        stage(AT_FWD1, forward1)
        stage(AT_FWD2, forward2)
        stage(AT_PASS, pass_sums)
        stage(0, send_own)

        @pl.when(t < 4)
        def _():
            send_grads(t)

        @pl.when(t == AT_SUM)
        def _():
            arrived(gnear, g_rs)
            for end in range(2):
                for c in range(2):
                    for p in range(4):
                        gsum[end, c * COLS:(c + 1) * COLS, p * TOK:(p + 1) * TOK] = (
                            gnear[end, c, p].T
                        )

        @pl.when(t == AT_FINISH)
        def _():
            mom_in.wait()

        stage(AT_SUM, make_sums)
        stage(AT_FINISH, finish)
        stage(AT_OWN1, tiles(own1))
        stage(AT_OWN2, tiles(own2))
        stage(AT_RELAY, tiles(relay))
        return 0

    lax.fori_loop(0, NQ + AT_RELAY, step, 0)

    pltpu.make_async_copy(nm_ref, nm_ref, nm_sem).wait()
    sent(gnear, g_ss)
    sent(abuf.at[pl.ds(0, 3 * NQ // 4)], raw_ss)
    sent(sout.at[pl.ds(0, NQ // 2)], sum_ss.at[0])
    sent(scout.at[pl.ds(0, NQ // 2)], sum_ss.at[1])
    sent(sbuf.at[pl.ds(0, NQ // 4)], pass_ss.at[0])
    sent(scin.at[pl.ds(0, NQ // 2)], pass_ss.at[1])

    def drain_tile(t, mine):
        @pl.when(owner(t) == me)
        def _():
            slot = lax.div(t, NDP)
            sent(sqs.at[slot, pl.ds(0, NZ - 1)], sq_ss.at[slot])
            sent(uall.at[pl.ds(0, NDP // 2 * 128)], up_ss.at[slot])

        @pl.when(lax.rem(owner(t), 2) != lax.rem(me, 2))
        def _():
            onward(t).wait_recv()

        return mine + jnp.where(owner(t) == me, 1, 0)

    mine = lax.fori_loop(0, NT, drain_tile, 0)
    whole = pltpu.make_async_copy(uall, upd_ref, ul_sem)
    whole.start()
    for n in (NT // NDP, SLOTS):
        @pl.when(mine == n)
        def _():
            sent(msg.at[pl.ds(0, NT - n)], msg_ss)
            sent(uall.at[pl.ds(0, (NT // 2 - n) * 128)], relay_ss)

    whole.wait()


def hand_out(nm_in, upd_in, nm_out, upd_out, nm_mid, upd_mid, sem):
    parts = [pl.ds(k * ROWS // 8, ROWS // 8) for k in range(8)]
    triples = [(nm_in, nm_mid, nm_out), (upd_in, upd_mid, upd_out)]

    def copy(i, j, way):
        return pltpu.make_async_copy(
            triples[i][way].at[parts[j]], triples[i][way + 1].at[parts[j]], sem.at[way, i, j]
        )

    every = [(i, j) for j in range(8) for i in range(2)]
    for i, j in every:
        copy(i, j, 0).start()
    for i, j in every:
        copy(i, j, 0).wait()
        copy(i, j, 1).start()
    for i, j in every:
        copy(i, j, 1).wait()


def body(momentum, activations, out_grads, positions):
    hbm = pl.BlockSpec(memory_space=pltpu.HBM)
    dma = pltpu.SemaphoreType.DMA
    new_momentum, update = pl.pallas_call(
        kernel,
        out_shape=(
            jax.ShapeDtypeStruct((ROWS, COLS), jnp.float32),
            jax.ShapeDtypeStruct((ROWS, COLS), jnp.bfloat16),
        ),
        in_specs=[hbm] * 5,
        out_specs=(hbm, hbm),
        scratch_shapes=[
            pltpu.VMEM((NZ * TOK, COLS), jnp.bfloat16),
            pltpu.VMEM((2, 4, ROWS), jnp.int32),
            pltpu.VMEM((2, COLS, 3 * COLS), jnp.bfloat16),
            pltpu.VMEM((NQ, 4, TOK, CHUNK), jnp.bfloat16),
            pltpu.VMEM((COLS, (NZ + 3) * TOK), jnp.bfloat16),
            pltpu.VMEM((2, 2, 4, TOK, COLS), jnp.bfloat16),
            pltpu.VMEM((2, 2 * COLS, 4 * TOK), jnp.bfloat16),
            pltpu.VMEM((ROWS, COLS), jnp.float32),
            pltpu.VMEM((NQ, CHUNK, COLS), jnp.float32),
            pltpu.VMEM((NQ, 2, COLS, CHUNK), jnp.int16),
            pltpu.VMEM((NQ, 8, 128), jnp.float32),
            pltpu.VMEM((NQ, 2, COLS, CHUNK), jnp.int16),
            pltpu.VMEM((NQ, 8, 128), jnp.float32),
            pltpu.VMEM((NT, 16, 128), jnp.float32),
            pltpu.VMEM((SLOTS, NDP, 16, 128), jnp.float32),
            pltpu.VMEM((SLOTS, COLS, 128), jnp.float32),
            pltpu.VMEM((SLOTS, NZ, 8, 128), jnp.float32),
            pltpu.VMEM((ROWS, COLS), jnp.bfloat16),
            dma, dma, dma, dma, dma((NQ, 4)),
            dma, dma,
            dma((2,)), dma((NQ, 2)), dma((2,)),
            dma, dma((SLOTS,)),
            dma((SLOTS,)), dma((SLOTS,)),
            dma((SLOTS,)), dma((NT,)), dma, dma, dma((3,)),
        ],
        compiler_params=pltpu.CompilerParams(
            collective_id=0, has_side_effects=True, vmem_limit_bytes=60 << 20
        ),
    )(activations, momentum[0], out_grads, positions[0], dct_blocks())
    shapes = (
        jax.ShapeDtypeStruct((ROWS, COLS), jnp.float32),
        jax.ShapeDtypeStruct((ROWS, COLS), jnp.bfloat16),
    )
    new_momentum, update = pl.pallas_call(
        hand_out,
        out_shape=shapes,
        in_specs=[hbm] * 2,
        out_specs=(hbm, hbm),
        scratch_shapes=[pltpu.VMEM(s.shape, s.dtype) for s in shapes] + [dma((2, 2, 8))],
        compiler_params=pltpu.CompilerParams(vmem_limit_bytes=62 << 20),
    )(new_momentum, update)
    return new_momentum[None], update


def solution(mesh):
    placed = (
        P("dp", None, "tensor"),
        P(("dp", "tensor"), None),
        P("dp", "tensor"),
        P("dp", "tensor", None, None),
    )
    return jax.shard_map(
        body,
        mesh=mesh,
        in_specs=placed,
        out_specs=(P("dp", None, "tensor"), P(None, "tensor")),
        check_vma=False,
    )
```

```python
import functools

import jax
import jax.numpy as jnp
import numpy as np
from jax import lax
from jax.experimental import pallas as pl
from jax.experimental.pallas import tpu as pltpu
from jax.sharding import PartitionSpec as P

MESH = pl.DeviceIdType.MESH
ROWS, COLS, TOK = 5120, 128, 128
NZ, NDP = 8, 32
CHUNK = 256
NQ = ROWS // CHUNK
TPC = CHUNK // 128
NT = ROWS // 128
SLOTS = -(-NT // NDP)

AT_FWD1, AT_FWD2, AT_SUM, AT_PASS, AT_FINISH = 3, 5, 7, 9, 11
AT_OWN1, AT_OWN2, AT_RELAY = 14, 19, 25


def dct_blocks():
    freq = np.arange(64, dtype=np.float64)[:, None]
    place = np.arange(64, dtype=np.float64)[None, :]
    scales = np.where(freq == 0, 1.0 / 8.0, np.sqrt(2.0 / 64.0))
    table = scales * np.cos(np.pi * (2.0 * place + 1.0) * freq / 128.0)
    blocks = np.kron(np.eye(COLS // 64), table)
    high = blocks.astype(jnp.bfloat16)
    low = (blocks - high.astype(np.float64)).astype(jnp.bfloat16)
    return np.stack([
        np.concatenate([high, high, low], axis=1),
        np.concatenate([high.T, high.T, low.T], axis=1),
    ])


def product(parts, x):
    high = x.astype(jnp.bfloat16)
    low = (x - high.astype(jnp.float32)).astype(jnp.bfloat16)
    return jnp.dot(
        parts, jnp.concatenate([high, low, high], axis=0), preferred_element_type=jnp.float32
    )


def kernel(
    a_ref, m_ref, g_ref, pos_hbm, dct_hbm,
    nm_ref, upd_ref,
    gall, pos_ref, dct_ref,
    abuf, gown, gnear, gsum, mbuf, nmbuf, sout, scout, sbuf, scin,
    msg, rx, dec, sqs, uall,
    loc_sem, m_sem, nm_sem, raw_ss, raw_rs, g_ss, g_rs,
    sum_ss, sum_rs, pass_ss, msg_ss, rx_rs, sq_ss, sq_rs, up_ss, up_rs, ul_sem, relay_ss, in_sem,
):
    me = lax.axis_index("dp")
    z = lax.axis_index("tensor")
    right = lax.rem(z + 1, NZ)
    left = lax.rem(z + NZ - 1, NZ)
    twin = me + 1 - 2 * lax.rem(me, 2)

    def place(q):
        return lax.rem(z + 4 - lax.rem(q, 4), 4)

    def cols(q):
        return pl.ds(pl.multiple_of(q * CHUNK, CHUNK), CHUNK)

    def owner(t):
        return lax.rem(t * 5, NDP)

    mom_in = pltpu.make_async_copy(m_ref, mbuf, m_sem)

    def mom_out(q):
        return pltpu.make_async_copy(nmbuf.at[q], nm_ref.at[cols(q)], nm_sem)

    def own_local(q):
        return pltpu.make_async_copy(a_ref.at[:, cols(q)], abuf.at[q, place(q)], loc_sem)

    def sent(ref, sem):
        pltpu.make_async_remote_copy(
            src_ref=ref, dst_ref=ref, send_sem=sem, recv_sem=sem,
            device_id={"tensor": right}, device_id_type=MESH,
        ).wait_send()

    def arrived(ref, sem):
        pltpu.make_async_remote_copy(
            src_ref=ref, dst_ref=ref, send_sem=sem, recv_sem=sem,
            device_id={"tensor": right}, device_id_type=MESH,
        ).wait_recv()

    def raw(q, p, way):
        return pltpu.make_async_remote_copy(
            src_ref=abuf.at[q, p],
            dst_ref=abuf.at[q, p],
            send_sem=raw_ss,
            recv_sem=raw_rs.at[q, p],
            device_id={"tensor": left if way else right},
            device_id_type=MESH,
        )

    def grads(end, c, p):
        target = lax.rem(z + (NZ - 1 - c if end else 1 + c), NZ)
        block = lax.rem(target + (NZ - 3 if end else 0) + p, NZ)
        return pltpu.make_async_remote_copy(
            src_ref=g_ref.at[pl.ds(pl.multiple_of(block * TOK, TOK), TOK)],
            dst_ref=gnear.at[end, c, p],
            send_sem=g_ss,
            recv_sem=g_rs,
            device_id={"tensor": target},
            device_id_type=MESH,
        )

    def sums(q, target):
        return (
            pltpu.make_async_remote_copy(
                src_ref=sout.at[q], dst_ref=sbuf.at[q],
                send_sem=sum_ss.at[0], recv_sem=sum_rs.at[q, 0],
                device_id={"tensor": target}, device_id_type=MESH,
            ),
            pltpu.make_async_remote_copy(
                src_ref=scout.at[q], dst_ref=scin.at[q],
                send_sem=sum_ss.at[1], recv_sem=sum_rs.at[q, 1],
                device_id={"tensor": target}, device_id_type=MESH,
            ),
        )

    def passed(q, target):
        return (
            pltpu.make_async_remote_copy(
                src_ref=sbuf.at[q, 1], dst_ref=sbuf.at[q, 1],
                send_sem=pass_ss.at[0], recv_sem=sum_rs.at[q, 0],
                device_id={"tensor": target}, device_id_type=MESH,
            ),
            pltpu.make_async_remote_copy(
                src_ref=scin.at[q], dst_ref=scin.at[q],
                send_sem=pass_ss.at[1], recv_sem=sum_rs.at[q, 1],
                device_id={"tensor": target}, device_id_type=MESH,
            ),
        )

    def picks(t, source, target):
        slot = lax.div(t, NDP)
        return pltpu.make_async_remote_copy(
            src_ref=msg.at[t], dst_ref=rx.at[slot, source],
            send_sem=msg_ss, recv_sem=rx_rs.at[slot],
            device_id={"dp": target}, device_id_type=MESH,
        )

    def squares(slot, source, target):
        return pltpu.make_async_remote_copy(
            src_ref=sqs.at[slot, z], dst_ref=sqs.at[slot, source],
            send_sem=sq_ss.at[slot], recv_sem=sq_rs.at[slot],
            device_id={"tensor": target}, device_id_type=MESH,
        )

    def tile(t):
        return pl.ds(pl.multiple_of(t * 128, 128), 128)

    def spread(t, target):
        slot = lax.div(t, NDP)
        return pltpu.make_async_remote_copy(
            src_ref=uall.at[tile(t)], dst_ref=uall.at[tile(t)],
            send_sem=up_ss.at[slot], recv_sem=up_rs.at[t],
            device_id={"dp": target}, device_id_type=MESH,
        )

    def onward(t):
        return pltpu.make_async_remote_copy(
            src_ref=uall.at[tile(t)], dst_ref=uall.at[tile(t)],
            send_sem=relay_ss, recv_sem=up_rs.at[t],
            device_id={"dp": twin}, device_id_type=MESH,
        )

    def keep(t):
        return pltpu.make_async_copy(uall.at[tile(t)], upd_ref.at[tile(t)], ul_sem)

    def start_own(q, _):
        own_local(q).start()
        return 0

    small = [
        pltpu.make_async_copy(source, target, in_sem.at[i])
        for i, (source, target) in enumerate(
            ((g_ref, gall), (pos_hbm, pos_ref), (dct_hbm, dct_ref))
        )
    ]
    for copy in small:
        copy.start()
    mom_in.start()
    lax.fori_loop(0, NQ, start_own, 0)
    barrier = pltpu.get_barrier_semaphore()

    def greet_z(d, _):
        pl.semaphore_signal(
            barrier, inc=1, device_id={"tensor": lax.rem(z + d, NZ)}, device_id_type=MESH
        )
        return 0

    def greet_dp(d, _):
        pl.semaphore_signal(
            barrier, inc=1, device_id={"dp": lax.rem(me + d, NDP)}, device_id_type=MESH
        )
        return 0

    lax.fori_loop(1, NZ, greet_z, 0)
    lax.fori_loop(1, NDP, greet_dp, 0)
    for copy in small:
        copy.wait()
    for b in range(NZ + 3):
        block = gall[(b % NZ) * TOK:(b % NZ + 1) * TOK, :]
        gown[:, b * TOK:(b + 1) * TOK] = block.T
    every = abuf.at[pl.ds(0, NQ // 4)]
    pltpu.make_async_copy(every, every, loc_sem).wait()
    pl.semaphore_wait(barrier, NZ + NDP - 2)

    def send_own(q):
        u = place(q)
        @pl.when(u <= 2)
        def _():
            raw(q, u, 0).start()

        @pl.when(u >= 1)
        def _():
            raw(q, u, 1).start()

    def send_grads(p):
        for c in range(2):
            for end in range(2):
                grads(end, c, p).start()

    def forward1(q):
        u = place(q)

        @pl.when((u == 1) | (u == 2))
        def _():
            raw(q, u - 1, 0).wait_recv()
            raw(q, u - 1, 0).start()
            raw(q, u + 1, 1).wait_recv()
            raw(q, u + 1, 1).start()

    def forward2(q):
        u = place(q)

        @pl.when(u == 2)
        def _():
            raw(q, 0, 0).wait_recv()
            raw(q, 0, 0).start()

        @pl.when(u == 1)
        def _():
            raw(q, 3, 1).wait_recv()
            raw(q, 3, 1).start()

    def make_sums(q):
        u = place(q)
        @pl.when((u == 0) | (u == 3))
        def _():
            for p in range(4):
                @pl.when(u != p)
                def _():
                    raw(q, p, 0).wait_recv()
            end = lax.div(u, 3)
            far = jnp.dot(
                gsum[end], abuf[q].reshape(4 * TOK, CHUNK), preferred_element_type=jnp.float32
            )
            for c in range(2):
                part = far[c * COLS:(c + 1) * COLS]
                top = jnp.maximum(jnp.max(jnp.abs(part), axis=0, keepdims=True), 1e-30)
                sout[q, c] = jnp.round(part * (32767.0 / top)).astype(jnp.int32).astype(jnp.int16)
                unit = top * (1.0 / 32767.0)
                for i in range(TPC):
                    scout[q, c * TPC + i:c * TPC + i + 1, :] = unit[:, i * 128:(i + 1) * 128]
            for copy in sums(q, lax.rem(z + NZ - 1 + 2 * end, NZ)):
                copy.start()

    def pass_sums(q):
        u = place(q)

        @pl.when((u == 0) | (u == 3))
        def _():
            end = lax.div(u, 3)
            for copy in sums(q, right):
                copy.wait_recv()
            for copy in passed(q, lax.rem(z + 1 + (NZ - 2) * end, NZ)):
                copy.start()

    def finish(q):
        u = place(q)
        inner = jnp.where((u == 1) | (u == 2), 1, 0)

        @pl.when(inner == 1)
        def _():
            for copy in passed(q, right):
                copy.wait_recv()

        first = lax.rem(z - u + NZ, NZ)
        near = jnp.dot(
            gown[:, pl.ds(pl.multiple_of(first * TOK, TOK), 4 * TOK)],
            abuf[q].reshape(4 * TOK, CHUNK),
            preferred_element_type=jnp.float32,
        )
        unit = jnp.concatenate(
            [scin[q, pl.ds(inner * TPC + i, 1), :] for i in range(TPC)], axis=1
        )
        accumulated = 0.9 * mbuf[cols(q), :].T + (near + sbuf[q, inner].astype(jnp.float32) * unit)
        coeffs = product(dct_ref[0], accumulated)
        lanes = lax.broadcasted_iota(jnp.int32, (64, CHUNK), 0)
        kept = []
        for b in range(2):
            block = coeffs[b * 64:(b + 1) * 64]
            tile_b = jnp.zeros((64, CHUNK), jnp.float32)
            for j in range(4):
                where = pos_ref[b, j:j + 1, cols(q)]
                value = jnp.where(where == lanes, block, 0.0)
                tile_b = tile_b + value
                total = jnp.sum(value, axis=0, keepdims=True)
                spot = where.astype(jnp.float32)
                row = b * 4 + j
                for i in range(TPC):
                    part = slice(i * 128, (i + 1) * 128)
                    msg[q * TPC + i, row:row + 1, :] = total[:, part]
                    msg[q * TPC + i, row + 8:row + 9, :] = spot[:, part]
            kept.append(tile_b)

        def hand_over(i, _):
            t = q * TPC + i

            @pl.when(owner(t) == me)
            def _():
                rx[lax.div(t, NDP), me] = msg[t]

            @pl.when(owner(t) != me)
            def _():
                picks(t, me, owner(t)).start()

            return 0

        lax.fori_loop(0, TPC, hand_over, 0)
        restored = product(dct_ref[1], jnp.concatenate(kept, axis=0))
        nmbuf[q] = (accumulated - restored).T
        mom_out(q).start()

    def own1(t):
        @pl.when(owner(t) == me)
        def _():
            slot = lax.div(t, NDP)

            arrived(rx.at[slot, pl.ds(0, NDP - 1)], rx_rs.at[slot])
            lanes = lax.broadcasted_iota(jnp.int32, (64, 128), 0).astype(jnp.float32)

            def add(s, totals):
                m = rx[slot, s]
                out = []
                for b in range(2):
                    total = totals[b]
                    for j in range(4):
                        row = b * 4 + j
                        total = total + jnp.where(
                            m[row + 8:row + 9] == lanes, m[row:row + 1], 0.0
                        )
                    out.append(total)
                return tuple(out)

            zero = jnp.zeros((64, 128), jnp.float32)
            summed = jnp.concatenate(
                lax.fori_loop(0, NDP, add, (zero, zero), unroll=8), axis=0
            )
            sqs[slot, z] = jnp.broadcast_to(
                jnp.sum(summed * summed, axis=0, keepdims=True), (8, 128)
            )

            def tell(d, _):
                squares(slot, z, lax.rem(z + d, NZ)).start()
                return 0

            lax.fori_loop(1, NZ, tell, 0)
            dec[slot] = product(dct_ref[1], summed)

    def own2(t):
        @pl.when(owner(t) == me)
        def _():
            slot = lax.div(t, NDP)

            arrived(sqs.at[slot, pl.ds(0, NZ - 1)], sq_rs.at[slot])
            total = sqs[slot, 0, 0:1]
            for s in range(1, NZ):
                total = total + sqs[slot, s, 0:1]
            scale = jnp.sqrt(total * (1.0 / (COLS * NZ)) + 1e-05)
            uall[tile(t), :] = (dec[slot] / scale).T.astype(jnp.bfloat16)

            def give(d, _):
                spread(t, lax.rem(me + 2 * d, NDP)).start()
                return 0

            lax.fori_loop(1, NDP // 2, give, 0)
            spread(t, twin).start()

    def relay(t):
        @pl.when((owner(t) != me) & (lax.rem(owner(t), 2) == lax.rem(me, 2)))
        def _():
            onward(t).wait_recv()
            onward(t).start()

    def step(t, _):
        def stage(at, act):
            @pl.when((t >= at) & (t < at + NQ))
            def _():
                act(t - at)

        def tiles(act):
            def run(q):
                def one(i, _):
                    act(q * TPC + i)
                    return 0
                lax.fori_loop(0, TPC, one, 0)
            return run

        stage(AT_FWD1, forward1)
        stage(AT_FWD2, forward2)
        stage(AT_PASS, pass_sums)
        stage(0, send_own)

        @pl.when(t < 4)
        def _():
            send_grads(t)

        @pl.when(t == AT_SUM)
        def _():
            arrived(gnear, g_rs)
            for end in range(2):
                for c in range(2):
                    for p in range(4):
                        gsum[end, c * COLS:(c + 1) * COLS, p * TOK:(p + 1) * TOK] = (
                            gnear[end, c, p].T
                        )

        @pl.when(t == AT_FINISH)
        def _():
            mom_in.wait()

        stage(AT_SUM, make_sums)
        stage(AT_FINISH, finish)
        stage(AT_OWN1, tiles(own1))
        stage(AT_OWN2, tiles(own2))
        stage(AT_RELAY, tiles(relay))
        return 0

    lax.fori_loop(0, NQ + AT_RELAY, step, 0)

    pltpu.make_async_copy(nm_ref, nm_ref, nm_sem).wait()
    sent(gnear, g_ss)
    sent(abuf.at[pl.ds(0, 3 * NQ // 4)], raw_ss)
    sent(sout.at[pl.ds(0, NQ // 2)], sum_ss.at[0])
    sent(scout.at[pl.ds(0, NQ // 2)], sum_ss.at[1])
    sent(sbuf.at[pl.ds(0, NQ // 4)], pass_ss.at[0])
    sent(scin.at[pl.ds(0, NQ // 2)], pass_ss.at[1])

    def drain_tile(t, mine):
        @pl.when(owner(t) == me)
        def _():
            slot = lax.div(t, NDP)
            sent(sqs.at[slot, pl.ds(0, NZ - 1)], sq_ss.at[slot])
            sent(uall.at[pl.ds(0, NDP // 2 * 128)], up_ss.at[slot])

        @pl.when(lax.rem(owner(t), 2) != lax.rem(me, 2))
        def _():
            onward(t).wait_recv()

        keep(t).start()
        return mine + jnp.where(owner(t) == me, 1, 0)

    mine = lax.fori_loop(0, NT, drain_tile, 0)
    whole = pltpu.make_async_copy(uall, upd_ref, ul_sem)
    for n in (NT // NDP, SLOTS):
        @pl.when(mine == n)
        def _():
            sent(msg.at[pl.ds(0, NT - n)], msg_ss)
            sent(uall.at[pl.ds(0, (NT // 2 - n) * 128)], relay_ss)

    whole.wait()


def hand_out(nm_in, upd_in, nm_out, upd_out, nm_mid, upd_mid, sem):
    parts = [pl.ds(k * ROWS // 8, ROWS // 8) for k in range(8)]
    triples = [(nm_in, nm_mid, nm_out), (upd_in, upd_mid, upd_out)]

    def copy(i, j, way):
        return pltpu.make_async_copy(
            triples[i][way].at[parts[j]], triples[i][way + 1].at[parts[j]], sem.at[way, i, j]
        )

    every = [(i, j) for j in range(8) for i in range(2)]
    for i, j in every:
        copy(i, j, 0).start()
    for i, j in every:
        copy(i, j, 0).wait()
        copy(i, j, 1).start()
    for i, j in every:
        copy(i, j, 1).wait()


def body(momentum, activations, out_grads, positions):
    hbm = pl.BlockSpec(memory_space=pltpu.HBM)
    dma = pltpu.SemaphoreType.DMA
    new_momentum, update = pl.pallas_call(
        kernel,
        out_shape=(
            jax.ShapeDtypeStruct((ROWS, COLS), jnp.float32),
            jax.ShapeDtypeStruct((ROWS, COLS), jnp.bfloat16),
        ),
        in_specs=[hbm] * 5,
        out_specs=(hbm, hbm),
        scratch_shapes=[
            pltpu.VMEM((NZ * TOK, COLS), jnp.bfloat16),
            pltpu.VMEM((2, 4, ROWS), jnp.int32),
            pltpu.VMEM((2, COLS, 3 * COLS), jnp.bfloat16),
            pltpu.VMEM((NQ, 4, TOK, CHUNK), jnp.bfloat16),
            pltpu.VMEM((COLS, (NZ + 3) * TOK), jnp.bfloat16),
            pltpu.VMEM((2, 2, 4, TOK, COLS), jnp.bfloat16),
            pltpu.VMEM((2, 2 * COLS, 4 * TOK), jnp.bfloat16),
            pltpu.VMEM((ROWS, COLS), jnp.float32),
            pltpu.VMEM((NQ, CHUNK, COLS), jnp.float32),
            pltpu.VMEM((NQ, 2, COLS, CHUNK), jnp.int16),
            pltpu.VMEM((NQ, 8, 128), jnp.float32),
            pltpu.VMEM((NQ, 2, COLS, CHUNK), jnp.int16),
            pltpu.VMEM((NQ, 8, 128), jnp.float32),
            pltpu.VMEM((NT, 16, 128), jnp.float32),
            pltpu.VMEM((SLOTS, NDP, 16, 128), jnp.float32),
            pltpu.VMEM((SLOTS, COLS, 128), jnp.float32),
            pltpu.VMEM((SLOTS, NZ, 8, 128), jnp.float32),
            pltpu.VMEM((ROWS, COLS), jnp.bfloat16),
            dma, dma, dma, dma, dma((NQ, 4)),
            dma, dma,
            dma((2,)), dma((NQ, 2)), dma((2,)),
            dma, dma((SLOTS,)),
            dma((SLOTS,)), dma((SLOTS,)),
            dma((SLOTS,)), dma((NT,)), dma, dma, dma((3,)),
        ],
        compiler_params=pltpu.CompilerParams(
            collective_id=0, has_side_effects=True, vmem_limit_bytes=60 << 20
        ),
    )(activations, momentum[0], out_grads, positions[0], dct_blocks())
    shapes = (
        jax.ShapeDtypeStruct((ROWS, COLS), jnp.float32),
        jax.ShapeDtypeStruct((ROWS, COLS), jnp.bfloat16),
    )
    new_momentum, update = pl.pallas_call(
        hand_out,
        out_shape=shapes,
        in_specs=[hbm] * 2,
        out_specs=(hbm, hbm),
        scratch_shapes=[pltpu.VMEM(s.shape, s.dtype) for s in shapes] + [dma((2, 2, 8))],
        compiler_params=pltpu.CompilerParams(vmem_limit_bytes=62 << 20),
    )(new_momentum, update)
    return new_momentum[None], update


def solution(mesh):
    placed = (
        P("dp", None, "tensor"),
        P(("dp", "tensor"), None),
        P("dp", "tensor"),
        P("dp", "tensor", None, None),
    )
    return jax.shard_map(
        body,
        mesh=mesh,
        in_specs=placed,
        out_specs=(P("dp", None, "tensor"), P(None, "tensor")),
        check_vma=False,
    )
```
